256 devices in a mesh: section: 2 (over core), hid: 16 (over x, z_hi), mod: 8 (over y, z_lo).
Axes of the slice: x: 4, y: 4, z: 8 (z_hi: 4, z_lo: 2; z = z_hi * 2 + z_lo), core: 2. Of those that a mesh axis runs over, the one named last changes fastest.
Arguments:
- tokens: float32 [4096, 5120], P(('section', 'hid'), 'mod'), may hold values from -200 to 200
- gain_first: float32 [5120], P('mod'), may hold values from 0.1 to 1.9
- gate_first: bfloat16 [5120, 13824], P('mod', 'hid'), may hold values from -0.078125 to 0.078125
- up_first: bfloat16 [5120, 13824], P('mod', 'hid'), may hold values from -0.078125 to 0.078125
- down_first: bfloat16 [13824, 5120], P('hid', 'mod'), may hold values from -0.0546875 to 0.0546875
- gain_second: float32 [5120], P('mod'), may hold values from 0.1 to 1.9
- gate_second: bfloat16 [5120, 13824], P('mod', ('section', 'hid')), may hold values from -0.078125 to 0.078125
- up_second: bfloat16 [5120, 13824], P('mod', ('section', 'hid')), may hold values from -0.078125 to 0.078125
- down_second: bfloat16 [13824, 5120], P(('section', 'hid'), 'mod'), may hold values from -0.0546875 to 0.0546875
Outputs:
- result: float32 [4096, 5120], P(('section', 'hid'), 'mod')
The draws below stay inside these ranges and needn't reach their ends.
All inputs are finite; a program needn't handle non-finite values.
Results may differ from the reference program's by a relative error of at most 0.006.
Values may be sent and summed in bfloat16 or wider, within the bound.
No kernel may reach another device: no remote copies, remote signals or barrier semaphores. Data moves between devices by JAX's collectives and lax.ppermute only.
A program may use at most 64 MiB of HBM per device.

```python
import jax
import jax.numpy as jnp
from jax import lax

D = 5120
FF = 13824
ROWS = 4096
N_SECTION = 2
N_HID = 16
N_MOD = 8


def draw_tokens(key, part):
    keys = jax.random.split(jax.random.fold_in(key, 7), 4)
    columns = jnp.arange(D, dtype=jnp.float32) / D
    col_scale = jnp.exp(jnp.log(3.0) * columns) * jnp.exp(jax.random.uniform(keys[0], (D,), jnp.float32, 0.0, jnp.log(3.3)))
    base = jnp.clip(jax.random.normal(keys[1], (ROWS, D), jnp.float32), -5.0, 5.0)
    row_scale = jnp.exp(jax.random.uniform(keys[3], (ROWS, 1), jnp.float32, jnp.log(0.3), jnp.log(3.0)))
    return base * row_scale * col_scale


def levels(own_key, dims, cuts, least, high):
    def one(dim, parts):
        steps = jax.random.uniform(jax.random.fold_in(jax.random.fold_in(own_key, 6), dim), (parts,), jnp.float32, least / len(cuts), high / len(cuts))
        return jnp.repeat(jnp.exp(steps), dims[dim] // parts).reshape((-1,) + (1,) * (len(dims) - dim - 1))

    level = one(*cuts[0])
    for cut in cuts[1:]:
        level = level * one(*cut)
    return level


def gaussian(rng, dims, scale, limit, cuts=(), held_as=jnp.bfloat16):
    level = levels(rng, dims, cuts, -0.22, 0.18) if cuts else 1.0
    entries = jax.random.normal(rng, dims, jnp.float32) * scale * level
    return jnp.minimum(jnp.maximum(entries, -limit), limit).astype(held_as)


def setup_inputs(seed: int = 0) -> dict:
    splits = jax.random.split(jax.random.key(seed), 10)
    return {
        "tokens": draw_tokens(jax.random.fold_in(splits[9], 71), 0),
        "gain_first": jnp.clip(1.0 + 0.18 * jax.random.normal(splits[1], (D,), jnp.float32), 0.1, 1.9),
        "gate_first": gaussian(splits[2], (D, FF), D ** -0.5, 0.078125, ((0, 8), (1, 16))),
        "up_first": gaussian(splits[3], (D, FF), D ** -0.5, 0.078125, ((0, 8), (1, 16))),
        "down_first": gaussian(splits[4], (FF, D), FF ** -0.5, 0.0546875, ((0, 16), (1, 8))),
        "gain_second": jnp.clip(1.0 + 0.18 * jax.random.normal(splits[5], (D,), jnp.float32), 0.1, 1.9),
        "gate_second": gaussian(splits[6], (D, FF), D ** -0.5, 0.078125, ((0, 8), (1, 32))),
        "up_second": gaussian(splits[7], (D, FF), D ** -0.5, 0.078125, ((0, 8), (1, 32))),
        "down_second": gaussian(splits[8], (FF, D), FF ** -0.5, 0.0546875, ((0, 32), (1, 8))),
    }


epsilon = 1e-06

def rounded_partial(normed, weight, first, block_width):
    product = jnp.dot(normed[:, first:first + block_width], weight[first:first + block_width, :], preferred_element_type=jnp.float32)
    return lax.optimization_barrier(product.astype(jnp.bfloat16)).astype(jnp.float32)

def apply_block(stream, gain, w_gate, w_up, w_down, down_groups):
    mean_sq = lax.optimization_barrier(jnp.mean(stream * stream, axis=1, keepdims=True))
    normed = (stream * lax.rsqrt(mean_sq + epsilon) * gain).astype(jnp.bfloat16)
    block_width = D // N_MOD
    gate_sum = jnp.zeros((stream.shape[0], w_gate.shape[1]), jnp.float32)
    up_sum = jnp.zeros((stream.shape[0], w_up.shape[1]), jnp.float32)
    for group in range(N_MOD):
        first = group * block_width
        gate_sum = gate_sum + rounded_partial(normed, w_gate, first, block_width)
        up_sum = up_sum + rounded_partial(normed, w_up, first, block_width)
    activated = (jax.nn.silu(gate_sum) * up_sum).astype(jnp.bfloat16)
    unit_width = FF // down_groups
    output = stream
    for group in range(down_groups):
        output = output + rounded_partial(activated, w_down, group * unit_width, unit_width)
    return output

def reference(tokens, gain_first, gate_first, up_first, down_first, gain_second, gate_second, up_second, down_second):
    middle = apply_block(tokens, gain_first, gate_first, up_first, down_first, N_HID)
    return apply_block(middle, gain_second, gate_second, up_second, down_second, N_SECTION * N_HID)
```

```python
import jax
import jax.numpy as jnp
from jax import lax
from jax.sharding import Mesh
from jax.sharding import PartitionSpec as P

D = 5120
RING = 4
AHEAD = (1, 3, 2)
epsilon = 1e-06
BF16 = jnp.bfloat16
F32 = jnp.float32


def shifted(x, axis, distance):
    size = lax.axis_size(axis)
    return lax.ppermute(x, axis, [(i, (i + distance) % size) for i in range(size)])


def after(x, *others):
    return lax.optimization_barrier((x, *others))[0]


def from_behind(x, axis):
    got = {d: shifted(x, axis, d) for d in AHEAD}
    return [x, got[1], got[2], got[3]]


def sums_to_owner(blocks, axis):
    got = [shifted(blocks[d].astype(BF16), axis, -d) for d in AHEAD]
    total = blocks[0]
    for g in got:
        total = total + g.astype(F32)
    return total


def whole_weights(own_up, own_down, other_core_up=None, order=()):
    half = own_down.shape[0]
    mine = from_behind(after(own_up, *order), "y")
    theirs = [shifted(w, "section", 1) for w in mine]
    gate = jnp.concatenate([jnp.concatenate([a[:, :half], b[:, :half]], 1) for a, b in zip(mine, theirs)], 0)
    up = jnp.concatenate([jnp.concatenate([a[:, half:], b[:, half:]], 1) for a, b in zip(mine, theirs)], 0)
    mine_down = from_behind(after(own_down, mine[1], mine[2], mine[3]), "y")
    theirs_down = [shifted(w, "section", 1) for w in mine_down]
    down = jnp.concatenate([jnp.concatenate([a, b], 0) for a, b in zip(mine_down, theirs_down)], 1)
    return (gate, up, down), mine_down[1:]


def product(a, b):
    return jnp.dot(a, b, preferred_element_type=F32)


def block(v, gains, weights):
    gate, up, down = weights
    rows = v[0].shape[0]
    half = rows // 2
    squares = sum(jnp.sum(s * s, axis=1, keepdims=True) for s in v)
    there = shifted(squares, "z_lo", 1)
    squares = squares + jnp.concatenate([there[half:], there[:half]], 0)
    scale = lax.rsqrt(squares / D + epsilon)
    normed = jnp.concatenate([(s * scale * g).astype(BF16) for s, g in zip(v, gains)], 1)

    def gathered(part):
        column = jnp.concatenate(from_behind(part, "z_hi"), 0)
        return jnp.concatenate(from_behind(column, "x"), 0)

    give = gathered(normed[half:])
    give_gate = product(give, gate).astype(BF16)
    give_up = product(give, up).astype(BF16)
    got_gate = shifted(give_gate, "z_lo", 1)
    got_up = shifted(give_up, "z_lo", 1)
    keep = gathered(normed[:half])
    gate_sum = product(keep, gate) + got_gate.astype(F32)
    up_sum = product(keep, up) + got_up.astype(F32)
    act_keep = (jax.nn.silu(gate_sum) * up_sum).astype(BF16)
    act_give = shifted(act_keep, "z_lo", 1)

    def returned(act):
        out = product(act, down)
        column = sums_to_owner(jnp.split(out, RING, 0), "x")
        return sums_to_owner(jnp.split(column, RING, 0), "z_hi")

    delta = jnp.concatenate([returned(act_keep), returned(act_give)], 0)
    width = v[0].shape[1]
    return [s + delta[:, d * width : (d + 1) * width] for d, s in enumerate(v)]


def per_device(
    tokens,
    gain_first,
    gate_first,
    up_first,
    down_first,
    gain_second,
    gate_second,
    up_second,
    down_second,
):
    core, y, z_lo = (lax.axis_index(a) for a in ("section", "y", "z_lo"))
    half = gate_second.shape[1]
    first = core == 0
    own_first = jnp.concatenate(
        [
            jnp.where(first, gate_first[:, :half], gate_first[:, half:]),
            jnp.where(first, up_first[:, :half], up_first[:, half:]),
        ],
        1,
    )
    own_down_first = lax.dynamic_slice_in_dim(down_first, core * half, half, 0)
    own_second = jnp.concatenate([gate_second, up_second], 1)

    rows = tokens.shape[0] // RING
    part = rows // 2
    gains = jnp.concatenate([gain_first[None], gain_second[None], jnp.zeros((6, gain_first.shape[0]), F32)], 0)

    def rows_of(owner):
        base = owner * rows
        mine = lax.dynamic_slice_in_dim(tokens, base + z_lo * part, part, 0)
        other = lax.dynamic_slice_in_dim(tokens, base + (1 - z_lo) * part, part, 0)
        return jnp.concatenate([mine, other, gains], 0)

    got = [rows_of(y)] + [None] * (RING - 1)
    for d in AHEAD:
        got[d] = shifted(rows_of((y + d) % RING), "y", d)
    v = [g[:rows] for g in got]
    gains_first = [g[rows : rows + 1] for g in got]
    gains_second = [g[rows + 1 : rows + 2] for g in got]

    weights_first, sent = whole_weights(own_first, own_down_first, order=got[1:])
    weights_second, _ = whole_weights(own_second, down_second, order=sent)

    v = block(v, gains_first, weights_first)
    v = block(v, gains_second, weights_second)

    result = jnp.zeros_like(tokens)
    for d in (0, *AHEAD):
        piece = v[d] if d == 0 else shifted(v[d], "y", -d)
        base = (y + d) % RING * rows
        result = lax.dynamic_update_slice_in_dim(result, piece[:part], base + z_lo * part, 0)
        result = lax.dynamic_update_slice_in_dim(result, piece[part:], base + (1 - z_lo) * part, 0)
    return result


def solution(mesh):
    axes = ("section", "x", "z_hi", "y", "z_lo")
    split = Mesh(mesh.devices.reshape(2, RING, RING, RING, 2), axes)
    hid, mod = ("x", "z_hi"), ("y", "z_lo")
    both = ("section", *hid)
    return jax.shard_map(
        per_device,
        mesh=split,
        in_specs=(
            P(both, mod),
            P(mod),
            P(mod, hid),
            P(mod, hid),
            P(hid, mod),
            P(mod),
            P(mod, both),
            P(mod, both),
            P(both, mod),
        ),
        out_specs=P(both, mod),
        check_vma=False,
    )
```

```python
import jax
import jax.numpy as jnp
from jax import lax
from jax.experimental import pallas as pl
from jax.sharding import Mesh
from jax.sharding import PartitionSpec as P

D = 5120
RING = 4
AHEAD = (2, 1, 3)
LANES = 128
epsilon = 1e-06
BF16 = jnp.bfloat16
F32 = jnp.float32


def shifted(x, axis, distance):
    size = lax.axis_size(axis)
    return lax.ppermute(x, axis, [(i, (i + distance) % size) for i in range(size)])


def after(x, *others):
    anywhere = pl.BlockSpec(memory_space=pl.ANY)
    return pl.pallas_call(
        lambda *refs: None,
        out_shape=jax.ShapeDtypeStruct(x.shape, x.dtype),
        in_specs=[anywhere] * (1 + len(others)),
        out_specs=anywhere,
        input_output_aliases={0: 0},
    )(x, *others)


def from_behind(x, axis):
    got = {d: shifted(x, axis, d) for d in AHEAD}
    return [x, got[1], got[2], got[3]]


def to_owners(x, axis):
    blocks = jnp.split(x, RING, 0)
    got = [blocks[0]] + [shifted(blocks[d], axis, -d) for d in AHEAD]
    return got, sum(g.astype(F32) for g in got)


def product(a, b):
    return jnp.dot(a, b, preferred_element_type=F32)


def three_pieces(x):
    high = lax.reduce_precision(x, 8, 7)
    middle = lax.reduce_precision(x - high, 8, 7)
    low = x - high - middle
    return [high.astype(BF16), middle.astype(BF16), low.astype(BF16)]


def message(v, gain):
    squares = jnp.sum(v * v, axis=1, keepdims=True)
    pieces = three_pieces(squares)
    blank = jnp.zeros((v.shape[0], LANES - len(pieces)), BF16)
    return jnp.concatenate([(v * gain).astype(BF16), *pieces, blank], 1)


def block(give, keep, gain, weights, down):
    depth = give.shape[1]
    units = weights[0].shape[1] // 2

    def partials(x):
        x = jnp.concatenate(x, 0)
        return [product(x[:, :depth], w) for w in weights], x[:, depth : depth + 3]

    sent_give = message(give, gain)
    sent_keep = message(keep, gain)
    column_give = from_behind(sent_give, "z_hi")
    column_keep = from_behind(after(sent_keep, *column_give[1:]), "z_hi")
    wide_give = from_behind(jnp.concatenate(column_give, 0), "x")
    parts_give, squares_give = partials(wide_give)
    given = jnp.concatenate([p.astype(BF16) for p in parts_give] + [squares_give], 1)
    wide_keep = from_behind(after(jnp.concatenate(column_keep, 0), given), "x")
    got = shifted(given, "z_lo", 1)
    parts_keep, squares_keep = partials(wide_keep)
    squares = jnp.sum(squares_keep.astype(F32), 1, keepdims=True) + jnp.sum(
        got[:, 4 * units :].astype(F32), 1, keepdims=True
    )
    scale = lax.rsqrt(squares / D + epsilon)
    act = []
    for j, own in enumerate(parts_keep):
        first = 2 * j * units
        gate_sum = scale * (own[:, :units] + got[:, first : first + units].astype(F32))
        up_sum = scale * (own[:, units:] + got[:, first + units : first + 2 * units].astype(F32))
        act.append((jax.nn.silu(gate_sum) * up_sum).astype(BF16))
    act_keep = jnp.concatenate(act, 1)
    act_give = shifted(act_keep, "z_lo", 1)
    out_keep = product(act_keep, down).astype(BF16)
    got_keep, column = to_owners(out_keep, "x")
    _, delta_keep = to_owners(column.astype(BF16), "z_hi")
    out_give = after(product(act_give, down).astype(BF16), *got_keep[1:])
    _, column = to_owners(out_give, "x")
    _, delta_give = to_owners(column.astype(BF16), "z_hi")
    return give + delta_give, keep + delta_keep


def per_device(
    tokens,
    gain_first,
    gate_first,
    up_first,
    down_first,
    gain_second,
    gate_second,
    up_second,
    down_second,
):
    core, z_lo = lax.axis_index("section"), lax.axis_index("z_lo")
    half = gate_second.shape[1]
    width = tokens.shape[1]
    rows = tokens.shape[0] // RING
    part = rows // 2

    def of_core(w):
        return jnp.where(core == 0, w[:, :half], w[:, half:])

    def whole(gate, up, down):
        both = lax.all_gather(jnp.concatenate([gate, up], 1), ("section", "y"), axis=0, tiled=True)
        lower = lax.all_gather(down, ("y", "section"), axis=0, tiled=True)
        return jnp.split(both, 2, 0), jnp.concatenate(jnp.split(lower, RING, 0), 1)

    weights_first, lower_first = whole(
        of_core(gate_first), of_core(up_first), lax.dynamic_slice_in_dim(down_first, core * half, half, 0)
    )
    weights_second, lower_second = whole(gate_second, up_second, down_second)

    gains = jnp.concatenate([gain_first[None], gain_second[None], jnp.zeros((6, width), F32)], 0)
    leaving = jnp.concatenate(
        [tokens.reshape(RING, rows, width), jnp.broadcast_to(gains[None], (RING, *gains.shape))], 1
    )
    came = jnp.concatenate(jnp.split(lax.all_to_all(leaving, "y", 0, 0, tiled=True), RING, 0), 2)[0]
    keep = lax.dynamic_slice_in_dim(came, z_lo * part, part, 0)
    give = lax.dynamic_slice_in_dim(came, (1 - z_lo) * part, part, 0)

    give, keep = block(give, keep, came[rows : rows + 1], weights_first, lower_first)
    keep, give = block(keep, give, came[rows + 1 : rows + 2], weights_second, lower_second)

    whole_rows = jnp.where(z_lo == 0, jnp.concatenate([keep, give], 0), jnp.concatenate([give, keep], 0))
    back = jnp.stack(jnp.split(whole_rows, RING, 1), 0)
    return lax.all_to_all(back, "y", 0, 0, tiled=True).reshape(tokens.shape)


def solution(mesh):
    axes = ("section", "x", "z_hi", "y", "z_lo")
    split = Mesh(mesh.devices.reshape(2, RING, RING, RING, 2), axes)
    hid, mod = ("x", "z_hi"), ("y", "z_lo")
    both = ("section", *hid)
    return jax.shard_map(
        per_device,
        mesh=split,
        in_specs=(
            P(both, mod),
            P(mod),
            P(mod, hid),
            P(mod, hid),
            P(hid, mod),
            P(mod),
            P(mod, both),
            P(mod, both),
            P(both, mod),
        ),
        out_specs=P(both, mod),
        check_vma=False,
    )
```

```python
import jax
import jax.numpy as jnp
from jax import lax
from jax.experimental import pallas as pl
from jax.sharding import Mesh
from jax.sharding import PartitionSpec as P

D = 5120
RING = 4
AHEAD = (2, 1, 3)
LANES = 128
epsilon = 1e-06
BF16 = jnp.bfloat16
F32 = jnp.float32


def shifted(x, axis, distance):
    size = lax.axis_size(axis)
    return lax.ppermute(x, axis, [(i, (i + distance) % size) for i in range(size)])


def after(x, *others):
    anywhere = pl.BlockSpec(memory_space=pl.ANY)
    return pl.pallas_call(
        lambda *refs: None,
        out_shape=jax.ShapeDtypeStruct(x.shape, x.dtype),
        in_specs=[anywhere] * (1 + len(others)),
        out_specs=anywhere,
        input_output_aliases={0: 0},
    )(x, *others)


def from_behind(x, axis):
    got = {d: shifted(x, axis, d) for d in AHEAD}
    return [x, got[1], got[2], got[3]]


def to_owners(x, axis):
    blocks = jnp.split(x, RING, 0)
    return [blocks[0]] + [shifted(blocks[d], axis, -d) for d in AHEAD]


def paired(x, axis, flip):
    return lax.ppermute(x, axis, [(i, i ^ flip) for i in range(RING)])


def column_of(x):
    two = jnp.concatenate([x, paired(x, "z_hi", 1)], 0)
    return jnp.concatenate([two, paired(two, "z_hi", 3)], 0)


def own_of_column(x):
    for flip in (3, 1):
        half = x.shape[0] // 2
        x = x[:half] + paired(x[half:].astype(BF16), "z_hi", flip).astype(F32)
    return x


def product(a, b):
    return jnp.dot(a, b, preferred_element_type=F32)


def three_pieces(x):
    high = lax.reduce_precision(x, 8, 7)
    middle = lax.reduce_precision(x - high, 8, 7)
    low = x - high - middle
    return [high.astype(BF16), middle.astype(BF16), low.astype(BF16)]


def message(v, gain):
    squares = jnp.sum(v * v, axis=1, keepdims=True)
    pieces = three_pieces(squares)
    blank = jnp.zeros((v.shape[0], LANES - len(pieces)), BF16)
    return jnp.concatenate([(v * gain).astype(BF16), *pieces, blank], 1)


def block(give, keep, gain, weights, lower, together):
    rows, depth = give.shape
    units = weights[0].shape[1] // 2

    def partials(x):
        x = jnp.concatenate(x, 0)
        return [product(x[:, :depth], w) for w in weights], x[:, depth : depth + 3]

    sent_give = message(give, gain)
    sent_keep = message(keep, gain)
    if together:
        column = column_of(jnp.concatenate([sent_give, sent_keep], 0)).reshape(RING, 2, rows, -1)
        column_give, column_keep = (column[:, i].reshape(RING * rows, -1) for i in range(2))
    else:
        column_give = column_of(sent_give)
        column_keep = column_of(sent_keep)
    wide_give = from_behind(column_give, "x")
    if together:
        wide_keep = from_behind(after(column_keep, *wide_give[1:]), "x")
    parts_give, squares_give = partials(wide_give)
    given = jnp.concatenate([p.astype(BF16) for p in parts_give] + [squares_give], 1)
    if not together:
        wide_keep = from_behind(after(column_keep, given), "x")
    got = shifted(given, "z_lo", 1)
    parts_keep, squares_keep = partials(wide_keep)
    lower = after(lower, *parts_keep)
    down = jnp.concatenate(jnp.split(lower, RING, 0), 1)
    squares = jnp.sum(squares_keep.astype(F32), 1, keepdims=True) + jnp.sum(
        got[:, 4 * units :].astype(F32), 1, keepdims=True
    )
    scale = lax.rsqrt(squares / D + epsilon)
    act = []
    for j, own in enumerate(parts_keep):
        first = 2 * j * units
        gate_sum = scale * (own[:, :units] + got[:, first : first + units].astype(F32))
        up_sum = scale * (own[:, units:] + got[:, first + units : first + 2 * units].astype(F32))
        act.append((jax.nn.silu(gate_sum) * up_sum).astype(BF16))
    act_keep = jnp.concatenate(act, 1)
    act_give = shifted(act_keep, "z_lo", 1)
    got_keep = to_owners(product(act_keep, down).astype(BF16), "x")
    out_give = product(act_give, down).astype(BF16)
    got_keep[2] = after(got_keep[2], out_give)
    out_give = after(out_give, got_keep[1], got_keep[3])
    delta_keep = own_of_column(sum(g.astype(F32) for g in got_keep))
    got_give = to_owners(out_give, "x")
    keep = keep + delta_keep
    got_give[2] = after(got_give[2], keep)
    delta_give = own_of_column(sum(g.astype(F32) for g in got_give))
    return give + delta_give, keep


def per_device(
    tokens,
    gain_first,
    gate_first,
    up_first,
    down_first,
    gain_second,
    gate_second,
    up_second,
    down_second,
):
    core, z_lo = lax.axis_index("section"), lax.axis_index("z_lo")
    half = gate_second.shape[1]
    width = tokens.shape[1]
    rows = tokens.shape[0] // RING
    part = rows // 2

    def of_core(w):
        return jnp.where(core == 0, w[:, :half], w[:, half:])

    def whole(gate, up, down):
        both = lax.all_gather(jnp.concatenate([gate, up], 1), ("section", "y"), axis=0, tiled=True)
        lower = lax.all_gather(down, ("y", "section"), axis=0, tiled=True)
        return jnp.split(both, 2, 0), lower

    weights_first, lower_first = whole(
        of_core(gate_first), of_core(up_first), lax.dynamic_slice_in_dim(down_first, core * half, half, 0)
    )
    weights_second, lower_second = whole(gate_second, up_second, down_second)

    gains = jnp.concatenate([gain_first[None], gain_second[None], jnp.zeros((6, width), F32)], 0)
    leaving = jnp.concatenate(
        [tokens.reshape(RING, rows, width), jnp.broadcast_to(gains[None], (RING, *gains.shape))], 1
    )
    came = jnp.concatenate(jnp.split(lax.all_to_all(leaving, "y", 0, 0, tiled=True), RING, 0), 2)[0]
    keep = lax.dynamic_slice_in_dim(came, z_lo * part, part, 0)
    give = lax.dynamic_slice_in_dim(came, (1 - z_lo) * part, part, 0)

    give, keep = block(give, keep, came[rows : rows + 1], weights_first, lower_first, True)
    keep, give = block(keep, give, came[rows + 1 : rows + 2], weights_second, lower_second, False)

    whole_rows = jnp.where(z_lo == 0, jnp.concatenate([keep, give], 0), jnp.concatenate([give, keep], 0))
    back = jnp.stack(jnp.split(whole_rows, RING, 1), 0)
    return lax.all_to_all(back, "y", 0, 0, tiled=True).reshape(tokens.shape)


def solution(mesh):
    axes = ("section", "x", "z_hi", "y", "z_lo")
    split = Mesh(mesh.devices.reshape(2, RING, RING, RING, 2), axes)
    hid, mod = ("x", "z_hi"), ("y", "z_lo")
    both = ("section", *hid)
    return jax.shard_map(
        per_device,
        mesh=split,
        in_specs=(
            P(both, mod),
            P(mod),
            P(mod, hid),
            P(mod, hid),
            P(hid, mod),
            P(mod),
            P(mod, both),
            P(mod, both),
            P(both, mod),
        ),
        out_specs=P(both, mod),
        check_vma=False,
    )
```

```python
import jax
import jax.numpy as jnp
from jax import lax
from jax.experimental import pallas as pl
from jax.experimental.pallas import tpu as pltpu
from jax.sharding import Mesh
from jax.sharding import PartitionSpec as P

D = 5120
RING = 4
AHEAD = (2, 1, 3)
LANES = 128
epsilon = 1e-06
BF16 = jnp.bfloat16
F32 = jnp.float32

MAIN, TAIL = 384, 48
UNITS = MAIN + TAIL
WIDE = 2 * UNITS
WIDE_PAD = 896
ACT_PAD = 512
SQUARES = 2 * TAIL
PIECES = 3
VMEM_BYTES = 24 * 1024 * 1024


def shifted(x, axis, distance):
    size = lax.axis_size(axis)
    return lax.ppermute(x, axis, [(i, (i + distance) % size) for i in range(size)])


def after(xs, *others):
    anywhere = pl.BlockSpec(memory_space=pl.ANY)
    return pl.pallas_call(
        lambda *refs: None,
        out_shape=[jax.ShapeDtypeStruct(x.shape, x.dtype) for x in xs],
        in_specs=[anywhere] * (len(xs) + len(others)),
        out_specs=[anywhere] * len(xs),
        input_output_aliases={i: i for i in range(len(xs))},
    )(*xs, *others)


def from_behind(x, axis):
    got = {d: shifted(x, axis, d) for d in AHEAD}
    return [x, got[1], got[2], got[3]]


def to_owners(blocks, axis):
    return [blocks[0]] + [shifted(blocks[d], axis, -d) for d in AHEAD]


def paired(x, axis, flip):
    return lax.ppermute(x, axis, [(i, i ^ flip) for i in range(RING)])


def column_of(x):
    two = jnp.concatenate([x, paired(x, "z_hi", 1)], 0)
    return jnp.concatenate([two, paired(two, "z_hi", 3)], 0)


def own_of_column(x):
    for flip in (3, 1):
        half = x.shape[0] // 2
        x = x[:half] + paired(x[half:].astype(BF16), "z_hi", flip).astype(F32)
    return x


def three_pieces(x):
    high = lax.reduce_precision(x, 8, 7)
    middle = lax.reduce_precision(x - high, 8, 7)
    low = x - high - middle
    return [high.astype(BF16), middle.astype(BF16), low.astype(BF16)]


def message(v, gain):
    squares = jnp.sum(v * v, axis=1, keepdims=True)
    pieces = three_pieces(squares)
    blank = jnp.zeros((v.shape[0], LANES), BF16)
    return jnp.concatenate(
        [(v * gain).astype(BF16), blank[:, :SQUARES], *pieces, blank[:, : LANES - SQUARES - PIECES]], 1
    )


IN_VMEM = pl.BlockSpec(memory_space=pltpu.VMEM)
IN_HBM = pl.BlockSpec(memory_space=pltpu.HBM)


def fetched(w_ref, held, sems):
    pieces, size, _ = held.shape
    copies = [
        pltpu.make_async_copy(w_ref.at[pl.ds(i * size, size)], held.at[i], sems.at[i]) for i in range(pieces)
    ]
    for copy in copies:
        copy.start()

    def wait(i):
        copies[i].wait()
        return held[i]

    return wait


def partials(blocks, weights):
    rows, width = blocks[0].shape
    total_rows = RING * rows
    step = weights.shape[1]
    depth = RING * step
    pieces = 2 * RING

    def kernel(*refs):
        x_refs, (w_ref, out_ref, held, x_all, total, sems) = refs[:RING], refs[RING:]
        piece = fetched(w_ref, held, sems)
        for d in range(RING):
            x_all[d * rows : (d + 1) * rows, :] = x_refs[d][...]
        lane = lax.broadcasted_iota(jnp.int32, (total_rows, LANES), 1)
        head = WIDE_PAD - LANES
        for j in range(2):
            for y in range(RING):
                term = lax.dot_general(
                    x_all[:, y * step : (y + 1) * step],
                    piece(j * RING + y),
                    (((1,), (1,)), ((), ())),
                    preferred_element_type=F32,
                )
                total[:, :WIDE] = term if y == 0 else total[:, :WIDE] + term
            first = j * WIDE_PAD
            out_ref[:, first : first + head] = total[:, :head].astype(BF16)
            other = x_all[:, depth:].astype(F32) if j else jnp.zeros((total_rows, LANES), F32)
            out_ref[:, first + head : first + WIDE_PAD] = jnp.where(lane < SQUARES, total[:, head:], other).astype(BF16)

    return pl.pallas_call(
        kernel,
        in_specs=[IN_VMEM] * RING + [IN_HBM],
        out_specs=IN_VMEM,
        out_shape=jax.ShapeDtypeStruct((total_rows, 2 * WIDE_PAD), BF16),
        scratch_shapes=[
            pltpu.VMEM((pieces, WIDE, step), BF16),
            pltpu.VMEM((total_rows, width), BF16),
            pltpu.VMEM((total_rows, WIDE_PAD), F32),
            pltpu.SemaphoreType.DMA((pieces,)),
        ],
        compiler_params=pltpu.CompilerParams(vmem_limit_bytes=VMEM_BYTES),
        cost_estimate=pl.CostEstimate(
            flops=4 * total_rows * depth * WIDE, bytes_accessed=weights.size * 2, transcendentals=0
        ),
    )(*blocks, pltpu.with_memory_space_constraint(weights, pltpu.HBM))


def down_terms(act_ref, piece, out_refs):
    rows, width = out_refs[0].shape
    width //= RING
    for y in range(RING):
        w = piece(y)
        out = jnp.dot(act_ref[:, :UNITS], w[:UNITS], preferred_element_type=F32)
        out += jnp.dot(act_ref[:, ACT_PAD : ACT_PAD + UNITS], w[UNITS:], preferred_element_type=F32)
        for d in range(RING):
            out_refs[d][:, y * width : (y + 1) * width] = out[d * rows : (d + 1) * rows].astype(BF16)


def down_call(kernel, operands, lower, results, transcendentals):
    rows = operands[0].shape[0]
    width = lower.shape[1]
    shapes = results + [jax.ShapeDtypeStruct((rows // RING, RING * width), BF16)] * RING
    return pl.pallas_call(
        kernel,
        in_specs=[IN_VMEM] * len(operands) + [IN_HBM],
        out_specs=[IN_VMEM] * len(shapes),
        out_shape=shapes,
        scratch_shapes=[pltpu.VMEM((RING, 2 * UNITS, width), BF16), pltpu.SemaphoreType.DMA((RING,))],
        compiler_params=pltpu.CompilerParams(vmem_limit_bytes=VMEM_BYTES),
        cost_estimate=pl.CostEstimate(
            flops=2 * rows * lower.size, bytes_accessed=lower.size * 2, transcendentals=transcendentals
        ),
    )(*operands, pltpu.with_memory_space_constraint(lower, pltpu.HBM))


def activated_down(kept, got, lower):
    rows = kept.shape[0]

    def kernel(kept_ref, got_ref, w_ref, act_ref, *refs):
        out_refs, (held, sems) = refs[:RING], refs[RING:]
        piece = fetched(w_ref, held, sems)

        def both(first, columns):
            part = pl.ds(first, columns)
            return kept_ref[:, part].astype(F32) + got_ref[:, part].astype(F32)

        head = WIDE_PAD - LANES
        last = both(WIDE_PAD + head, LANES)
        lane = lax.broadcasted_iota(jnp.int32, last.shape, 1)
        carried = (lane >= SQUARES) & (lane < SQUARES + PIECES)
        squares = jnp.sum(jnp.where(carried, last, 0.0), axis=1, keepdims=True)
        scale = lax.rsqrt(squares / D + epsilon)

        def unit(gate, up):
            gate = gate * scale
            return gate / (1.0 + jnp.exp(-gate)) * (up * scale)

        for j in range(2):
            first, place = j * WIDE_PAD, j * ACT_PAD
            act_ref[:, place : place + MAIN] = unit(both(first, MAIN), both(first + MAIN, MAIN)).astype(BF16)
            tile = last if j else both(head, LANES)
            tails = unit(tile, pltpu.roll(tile, LANES - TAIL, 1))
            act_ref[:, place + MAIN : place + ACT_PAD] = jnp.where(lane < TAIL, tails, 0.0).astype(BF16)
        down_terms(act_ref, piece, out_refs)

    act, *out = down_call(
        kernel, [kept, got], lower, [jax.ShapeDtypeStruct((rows, 2 * ACT_PAD), BF16)], rows * WIDE
    )
    return act, out


def down_product(act, lower):
    def kernel(act_ref, w_ref, *refs):
        out_refs, (held, sems) = refs[:RING], refs[RING:]
        down_terms(act_ref, fetched(w_ref, held, sems), out_refs)

    return list(down_call(kernel, [act], lower, [], 0))


def block(give, keep, gain, weights, lower, last):
    sent_give = message(give, gain)
    sent_keep = message(keep, gain)
    column_give = column_of(sent_give)
    column_keep = column_of(sent_keep)
    wide_give = from_behind(column_give, "x")
    given = partials(wide_give, weights)
    (column_keep,) = after([column_keep], *([given] if last else wide_give[1:]))
    wide_keep = from_behind(column_keep, "x")
    got = shifted(given, "z_lo", 1)
    kept = partials(wide_keep, weights)
    (lower,) = after([pltpu.with_memory_space_constraint(lower, pltpu.HBM)], kept[:16, :LANES])
    act_keep, out_keep = activated_down(kept, got, lower)
    act_give = shifted(act_keep, "z_lo", 1)
    got_keep = to_owners(out_keep, "x")
    out_give = down_product(act_give, lower)
    (got_keep[2],) = after([got_keep[2]], out_give[0])
    out_give[1:] = after(out_give[1:], got_keep[1], got_keep[3])
    keep = keep + own_of_column(sum(g.astype(F32) for g in got_keep))
    got_give = to_owners(out_give, "x")
    if not last:
        (got_give[2],) = after([got_give[2]], keep)
    give = give + own_of_column(sum(g.astype(F32) for g in got_give))
    return give, keep


def stacked(gate, up, first):
    def kernel(first_ref, gate_ref, up_ref, out_ref, sems):
        start = pl.multiple_of(first_ref[0], 16)
        copies = []
        place = 0
        for skip, size in ((0, MAIN), (MAIN, TAIL)):
            for ref in (gate_ref, up_ref):
                copies.append(
                    pltpu.make_async_copy(
                        ref.at[pl.ds(start + skip, size)], out_ref.at[pl.ds(place, size)], sems.at[len(copies)]
                    )
                )
                place += size
        for copy in copies:
            copy.start()
        for copy in copies:
            copy.wait()

    anywhere = pl.BlockSpec(memory_space=pltpu.HBM)
    return pl.pallas_call(
        kernel,
        in_specs=[pl.BlockSpec(memory_space=pltpu.SMEM), anywhere, anywhere],
        out_specs=anywhere,
        out_shape=jax.ShapeDtypeStruct((WIDE, gate.shape[1]), BF16),
        scratch_shapes=[pltpu.SemaphoreType.DMA((4,))],
    )(first.astype(jnp.int32).reshape(1), *(pltpu.with_memory_space_constraint(w, pltpu.HBM) for w in (gate, up)))


def per_device(
    tokens,
    gain_first,
    gate_first,
    up_first,
    down_first,
    gain_second,
    gate_second,
    up_second,
    down_second,
):
    core, z_lo = lax.axis_index("section"), lax.axis_index("z_lo")
    width = tokens.shape[1]
    rows = tokens.shape[0] // RING
    part = rows // 2

    gains = jnp.concatenate([gain_first[None], gain_second[None], jnp.zeros((6, width), F32)], 0)
    leaving = jnp.concatenate(
        [tokens.reshape(RING, rows, width), jnp.broadcast_to(gains[None], (RING, *gains.shape))], 1
    )
    came = jnp.concatenate(jnp.split(lax.all_to_all(leaving, "y", 0, 0, tiled=True), RING, 0), 2)[0]
    keep = lax.dynamic_slice_in_dim(came, z_lo * part, part, 0)
    give = lax.dynamic_slice_in_dim(came, (1 - z_lo) * part, part, 0)

    def whole(upper, down):
        return (
            lax.all_gather(upper, ("section", "y"), axis=0, tiled=True),
            lax.all_gather(down, ("y", "section"), axis=0, tiled=True),
        )

    first = core * UNITS
    lower_first = lax.dynamic_slice_in_dim(down_first, first, UNITS, 0)
    weights_first = whole(stacked(gate_first.T, up_first.T, first), lower_first)
    weights_second = whole(stacked(gate_second.T, up_second.T, jnp.zeros_like(first)), down_second)

    give, keep = block(give, keep, came[rows : rows + 1], *weights_first, False)
    keep, give = block(keep, give, came[rows + 1 : rows + 2], *weights_second, True)

    whole_rows = jnp.where(z_lo == 0, jnp.concatenate([keep, give], 0), jnp.concatenate([give, keep], 0))
    back = jnp.stack(jnp.split(whole_rows, RING, 1), 0)
    return lax.all_to_all(back, "y", 0, 0, tiled=True).reshape(tokens.shape)


def solution(mesh):
    axes = ("section", "x", "z_hi", "y", "z_lo")
    split = Mesh(mesh.devices.reshape(2, RING, RING, RING, 2), axes)
    hid, mod = ("x", "z_hi"), ("y", "z_lo")
    both = ("section", *hid)
    return jax.shard_map(
        per_device,
        mesh=split,
        in_specs=(
            P(both, mod),
            P(mod),
            P(mod, hid),
            P(mod, hid),
            P(hid, mod),
            P(mod),
            P(mod, both),
            P(mod, both),
            P(both, mod),
        ),
        out_specs=P(both, mod),
        check_vma=False,
    )
```

```python
import jax
import jax.numpy as jnp
from jax import lax
from jax.experimental import pallas as pl
from jax.experimental.pallas import tpu as pltpu
from jax.sharding import Mesh
from jax.sharding import PartitionSpec as P

D = 5120
RING = 4
AHEAD = (2, 1, 3)
LANES = 128
epsilon = 1e-06
BF16 = jnp.bfloat16
F32 = jnp.float32

MAIN, TAIL = 384, 48
UNITS = MAIN + TAIL
WIDE = 2 * UNITS
WIDE_PAD = 896
ACT_PAD = 512
SQUARES = 2 * TAIL
PIECES = 3
VMEM_BYTES = 24 * 1024 * 1024


def shifted(x, axis, distance):
    size = lax.axis_size(axis)
    return lax.ppermute(x, axis, [(i, (i + distance) % size) for i in range(size)])


def after(xs, *others):
    anywhere = pl.BlockSpec(memory_space=pl.ANY)
    return pl.pallas_call(
        lambda *refs: None,
        out_shape=[jax.ShapeDtypeStruct(x.shape, x.dtype) for x in xs],
        in_specs=[anywhere] * (len(xs) + len(others)),
        out_specs=[anywhere] * len(xs),
        input_output_aliases={i: i for i in range(len(xs))},
    )(*xs, *others)


def from_behind(x, axis):
    got = {d: shifted(x, axis, d) for d in AHEAD}
    return [x, got[1], got[2], got[3]]


def to_owners(blocks, axis):
    return [blocks[0]] + [shifted(blocks[d], axis, -d) for d in AHEAD]


def paired(x, axis, flip):
    return lax.ppermute(x, axis, [(i, i ^ flip) for i in range(RING)])


def doubled(x, flip):
    return jnp.concatenate([x, paired(x, "z_hi", flip)], 0)


def halved(x, flip):
    half = x.shape[0] // 2
    return x[:half] + paired(x[half:].astype(BF16), "z_hi", flip).astype(F32)


def three_pieces(x):
    high = lax.reduce_precision(x, 8, 7)
    middle = lax.reduce_precision(x - high, 8, 7)
    low = x - high - middle
    return [high.astype(BF16), middle.astype(BF16), low.astype(BF16)]


def message(v, gain):
    squares = jnp.sum(v * v, axis=1, keepdims=True)
    pieces = three_pieces(squares)
    blank = jnp.zeros((v.shape[0], LANES), BF16)
    return jnp.concatenate(
        [(v * gain).astype(BF16), blank[:, :SQUARES], *pieces, blank[:, : LANES - SQUARES - PIECES]], 1
    )


IN_VMEM = pl.BlockSpec(memory_space=pltpu.VMEM)
IN_HBM = pl.BlockSpec(memory_space=pltpu.HBM)


def fetched(w_ref, held, sems):
    pieces, size, _ = held.shape
    copies = [
        pltpu.make_async_copy(w_ref.at[pl.ds(i * size, size)], held.at[i], sems.at[i]) for i in range(pieces)
    ]
    for copy in copies:
        copy.start()

    def wait(i):
        copies[i].wait()
        return held[i]

    return wait


def partials(blocks, weights):
    rows, width = blocks[0].shape
    total_rows = RING * rows
    step = weights.shape[1]
    depth = RING * step
    pieces = 2 * RING

    def kernel(*refs):
        x_refs, (w_ref, out_ref, held, x_all, total, sems) = refs[:RING], refs[RING:]
        piece = fetched(w_ref, held, sems)
        for d in range(RING):
            x_all[d * rows : (d + 1) * rows, :] = x_refs[d][...]
        lane = lax.broadcasted_iota(jnp.int32, (total_rows, LANES), 1)
        head = WIDE_PAD - LANES
        for j in range(2):
            for y in range(RING):
                term = lax.dot_general(
                    x_all[:, y * step : (y + 1) * step],
                    piece(j * RING + y),
                    (((1,), (1,)), ((), ())),
                    preferred_element_type=F32,
                )
                total[:, :WIDE] = term if y == 0 else total[:, :WIDE] + term
            first = j * WIDE_PAD
            out_ref[:, first : first + head] = total[:, :head].astype(BF16)
            other = x_all[:, depth:].astype(F32) if j else jnp.zeros((total_rows, LANES), F32)
            out_ref[:, first + head : first + WIDE_PAD] = jnp.where(lane < SQUARES, total[:, head:], other).astype(BF16)

    return pl.pallas_call(
        kernel,
        in_specs=[IN_VMEM] * RING + [IN_HBM],
        out_specs=IN_VMEM,
        out_shape=jax.ShapeDtypeStruct((total_rows, 2 * WIDE_PAD), BF16),
        scratch_shapes=[
            pltpu.VMEM((pieces, WIDE, step), BF16),
            pltpu.VMEM((total_rows, width), BF16),
            pltpu.VMEM((total_rows, WIDE_PAD), F32),
            pltpu.SemaphoreType.DMA((pieces,)),
        ],
        compiler_params=pltpu.CompilerParams(vmem_limit_bytes=VMEM_BYTES),
        cost_estimate=pl.CostEstimate(
            flops=4 * total_rows * depth * WIDE, bytes_accessed=weights.size * 2, transcendentals=0
        ),
    )(*blocks, pltpu.with_memory_space_constraint(weights, pltpu.HBM))


def down_terms(act_ref, piece, out_refs):
    rows, width = out_refs[0].shape
    width //= RING
    for y in range(RING):
        w = piece(y)
        out = jnp.dot(act_ref[:, :UNITS], w[:UNITS], preferred_element_type=F32)
        out += jnp.dot(act_ref[:, ACT_PAD : ACT_PAD + UNITS], w[UNITS:], preferred_element_type=F32)
        for d in range(RING):
            out_refs[d][:, y * width : (y + 1) * width] = out[d * rows : (d + 1) * rows].astype(BF16)


def down_call(kernel, operands, lower, results, transcendentals):
    rows = operands[0].shape[0]
    width = lower.shape[1]
    shapes = results + [jax.ShapeDtypeStruct((rows // RING, RING * width), BF16)] * RING
    return pl.pallas_call(
        kernel,
        in_specs=[IN_VMEM] * len(operands) + [IN_HBM],
        out_specs=[IN_VMEM] * len(shapes),
        out_shape=shapes,
        scratch_shapes=[pltpu.VMEM((RING, 2 * UNITS, width), BF16), pltpu.SemaphoreType.DMA((RING,))],
        compiler_params=pltpu.CompilerParams(vmem_limit_bytes=VMEM_BYTES),
        cost_estimate=pl.CostEstimate(
            flops=2 * rows * lower.size, bytes_accessed=lower.size * 2, transcendentals=transcendentals
        ),
    )(*operands, pltpu.with_memory_space_constraint(lower, pltpu.HBM))


def activated_down(kept, got, lower):
    rows = kept.shape[0]

    def kernel(kept_ref, got_ref, w_ref, act_ref, *refs):
        out_refs, (held, sems) = refs[:RING], refs[RING:]
        piece = fetched(w_ref, held, sems)

        def both(first, columns):
            part = pl.ds(first, columns)
            return kept_ref[:, part].astype(F32) + got_ref[:, part].astype(F32)

        head = WIDE_PAD - LANES
        last = both(WIDE_PAD + head, LANES)
        lane = lax.broadcasted_iota(jnp.int32, last.shape, 1)
        carried = (lane >= SQUARES) & (lane < SQUARES + PIECES)
        squares = jnp.sum(jnp.where(carried, last, 0.0), axis=1, keepdims=True)
        scale = lax.rsqrt(squares / D + epsilon)

        def unit(gate, up):
            gate = gate * scale
            return gate / (1.0 + jnp.exp(-gate)) * (up * scale)

        for j in range(2):
            first, place = j * WIDE_PAD, j * ACT_PAD
            act_ref[:, place : place + MAIN] = unit(both(first, MAIN), both(first + MAIN, MAIN)).astype(BF16)
            tile = last if j else both(head, LANES)
            tails = unit(tile, pltpu.roll(tile, LANES - TAIL, 1))
            act_ref[:, place + MAIN : place + ACT_PAD] = jnp.where(lane < TAIL, tails, 0.0).astype(BF16)
        down_terms(act_ref, piece, out_refs)

    act, *out = down_call(
        kernel, [kept, got], lower, [jax.ShapeDtypeStruct((rows, 2 * ACT_PAD), BF16)], rows * WIDE
    )
    return act, out


def down_product(act, lower):
    def kernel(act_ref, w_ref, *refs):
        out_refs, (held, sems) = refs[:RING], refs[RING:]
        down_terms(act_ref, fetched(w_ref, held, sems), out_refs)

    return list(down_call(kernel, [act], lower, [], 0))


def block(column_give, keep, weights, lower, last):
    wide_give = from_behind(column_give, "x")
    given = partials(wide_give, weights)
    (column_keep,) = after([keep()], *([given] if last else wide_give[1:]))
    wide_keep = from_behind(column_keep, "x")
    got = shifted(given, "z_lo", 1)
    kept = partials(wide_keep, weights)
    (lower,) = after([pltpu.with_memory_space_constraint(lower, pltpu.HBM)], kept[:16, :LANES])
    act_keep, out_keep = activated_down(kept, got, lower)
    act_give = shifted(act_keep, "z_lo", 1)
    got_keep = to_owners(out_keep, "x")
    out_give = down_product(act_give, lower)
    (got_keep[2],) = after([got_keep[2]], out_give[0])
    got_give = to_owners(out_give, "x")
    return [sum(g.astype(F32) for g in got_keep), got_give]


def two_blocks(give, keep, gains, weights):
    column_keep, got_give = block(
        doubled(doubled(message(give, gains[0]), 1), 3),
        lambda: doubled(doubled(message(keep, gains[0]), 1), 3),
        *weights[0],
        False,
    )
    (rest,) = after([halved(column_keep, 3)], got_give[1])
    keep = keep + halved(rest, 1)
    (got_give[2],) = after([got_give[2]], keep)
    rest = halved(sum(g.astype(F32) for g in got_give), 3)
    two = doubled(message(keep, gains[1]), 1)
    (rest,) = after([rest], two)
    column = doubled(two, 3)
    give = give + halved(rest, 1)
    column_give, got_keep = block(
        column, lambda: doubled(doubled(message(give, gains[1]), 1), 3), *weights[1], True
    )
    give = give + halved(halved(column_give, 3), 1)
    keep = keep + halved(halved(sum(g.astype(F32) for g in got_keep), 3), 1)
    return give, keep


def stacked(gate, up, first):
    def kernel(first_ref, gate_ref, up_ref, out_ref):
        place = 0
        for skip, size in ((0, MAIN), (MAIN, TAIL)):
            for ref in (gate_ref, up_ref):
                out_ref[place : place + size, :] = ref[pl.ds(pl.multiple_of(first_ref[0] + skip, 16), size), :]
                place += size

    return pl.pallas_call(
        kernel,
        in_specs=[pl.BlockSpec(memory_space=pltpu.SMEM), IN_VMEM, IN_VMEM],
        out_specs=IN_VMEM,
        out_shape=jax.ShapeDtypeStruct((WIDE, gate.shape[1]), BF16),
        compiler_params=pltpu.CompilerParams(vmem_limit_bytes=VMEM_BYTES),
    )(first.astype(jnp.int32).reshape(1), gate, up)


def per_device(
    tokens,
    gain_first,
    gate_first,
    up_first,
    down_first,
    gain_second,
    gate_second,
    up_second,
    down_second,
):
    core, z_lo = lax.axis_index("section"), lax.axis_index("z_lo")
    width = tokens.shape[1]
    rows = tokens.shape[0] // RING
    part = rows // 2

    gains = jnp.concatenate([gain_first[None], gain_second[None], jnp.zeros((6, width), F32)], 0)
    leaving = jnp.concatenate(
        [tokens.reshape(RING, rows, width), jnp.broadcast_to(gains[None], (RING, *gains.shape))], 1
    )
    came = jnp.concatenate(jnp.split(lax.all_to_all(leaving, "y", 0, 0, tiled=True), RING, 0), 2)[0]
    keep = lax.dynamic_slice_in_dim(came, z_lo * part, part, 0)
    give = lax.dynamic_slice_in_dim(came, (1 - z_lo) * part, part, 0)

    def whole(upper, down):
        return (
            lax.all_gather(upper, ("section", "y"), axis=0, tiled=True),
            lax.all_gather(down, ("y", "section"), axis=0, tiled=True),
        )

    first = core * UNITS
    lower_first = lax.dynamic_slice_in_dim(down_first, first, UNITS, 0)
    weights_first = whole(stacked(gate_first.T, up_first.T, first), lower_first)
    weights_second = whole(stacked(gate_second.T, up_second.T, jnp.zeros_like(first)), down_second)

    gains = came[rows : rows + 1], came[rows + 1 : rows + 2]
    give, keep = two_blocks(give, keep, gains, (weights_first, weights_second))

    whole_rows = jnp.where(z_lo == 0, jnp.concatenate([keep, give], 0), jnp.concatenate([give, keep], 0))
    back = jnp.stack(jnp.split(whole_rows, RING, 1), 0)
    return lax.all_to_all(back, "y", 0, 0, tiled=True).reshape(tokens.shape)


def solution(mesh):
    axes = ("section", "x", "z_hi", "y", "z_lo")
    split = Mesh(mesh.devices.reshape(2, RING, RING, RING, 2), axes)
    hid, mod = ("x", "z_hi"), ("y", "z_lo")
    both = ("section", *hid)
    return jax.shard_map(
        per_device,
        mesh=split,
        in_specs=(
            P(both, mod),
            P(mod),
            P(mod, hid),
            P(mod, hid),
            P(hid, mod),
            P(mod),
            P(mod, both),
            P(mod, both),
            P(both, mod),
        ),
        out_specs=P(both, mod),
        check_vma=False,
    )
```

```python
import jax
import jax.numpy as jnp
from jax import lax
from jax.experimental import pallas as pl
from jax.experimental.pallas import tpu as pltpu
from jax.sharding import Mesh
from jax.sharding import PartitionSpec as P

D = 5120
RING = 4
AHEAD = (2, 1, 3)
LANES = 128
epsilon = 1e-06
BF16 = jnp.bfloat16
F32 = jnp.float32

MAIN, TAIL = 384, 48
UNITS = MAIN + TAIL
WIDE = 2 * UNITS
WIDE_PAD = 896
ACT_PAD = 512
SQUARES = 2 * TAIL
PIECES = 3
VMEM_BYTES = 24 * 1024 * 1024


def shifted(x, axis, distance):
    size = lax.axis_size(axis)
    return lax.ppermute(x, axis, [(i, (i + distance) % size) for i in range(size)])


def after(xs, *others):
    anywhere = pl.BlockSpec(memory_space=pl.ANY)
    return pl.pallas_call(
        lambda *refs: None,
        out_shape=[jax.ShapeDtypeStruct(x.shape, x.dtype) for x in xs],
        in_specs=[anywhere] * (len(xs) + len(others)),
        out_specs=[anywhere] * len(xs),
        input_output_aliases={i: i for i in range(len(xs))},
    )(*xs, *others)


def from_behind(x, axis):
    got = {d: shifted(x, axis, d) for d in AHEAD}
    return [x, got[1], got[2], got[3]]


def to_owners(blocks, axis):
    return [blocks[0]] + [shifted(blocks[d], axis, -d) for d in AHEAD]


def paired(x, axis, flip):
    return lax.ppermute(x, axis, [(i, i ^ flip) for i in range(RING)])


def doubled(x, flip):
    return jnp.concatenate([x, paired(x, "z_hi", flip)], 0)


def halved(x, flip):
    half = x.shape[0] // 2
    return x[:half] + paired(x[half:].astype(BF16), "z_hi", flip).astype(F32)


def three_pieces(x):
    high = lax.reduce_precision(x, 8, 7)
    middle = lax.reduce_precision(x - high, 8, 7)
    low = x - high - middle
    return [high.astype(BF16), middle.astype(BF16), low.astype(BF16)]


def message(v, gain):
    squares = jnp.sum(v * v, axis=1, keepdims=True)
    pieces = three_pieces(squares)
    blank = jnp.zeros((v.shape[0], LANES), BF16)
    return jnp.concatenate(
        [(v * gain).astype(BF16), blank[:, :SQUARES], *pieces, blank[:, : LANES - SQUARES - PIECES]], 1
    )


IN_VMEM = pl.BlockSpec(memory_space=pltpu.VMEM)
IN_HBM = pl.BlockSpec(memory_space=pltpu.HBM)


def fetched(w_ref, held, sems):
    pieces, size, _ = held.shape
    copies = [
        pltpu.make_async_copy(w_ref.at[pl.ds(i * size, size)], held.at[i], sems.at[i]) for i in range(pieces)
    ]
    for copy in copies:
        copy.start()

    def wait(i):
        copies[i].wait()
        return held[i]

    return wait


def partials(blocks, weights):
    rows, width = blocks[0].shape
    total_rows = RING * rows
    step = weights.shape[1]
    depth = RING * step
    pieces = 2 * RING

    def kernel(*refs):
        x_refs, (w_ref, out_ref, held, x_all, total, sems) = refs[:RING], refs[RING:]
        piece = fetched(w_ref, held, sems)
        for d in range(RING):
            x_all[d * rows : (d + 1) * rows, :] = x_refs[d][...]
        lane = lax.broadcasted_iota(jnp.int32, (total_rows, LANES), 1)
        head = WIDE_PAD - LANES
        for j in range(2):
            for y in range(RING):
                term = lax.dot_general(
                    x_all[:, y * step : (y + 1) * step],
                    piece(j * RING + y),
                    (((1,), (1,)), ((), ())),
                    preferred_element_type=F32,
                )
                total[:, :WIDE] = term if y == 0 else total[:, :WIDE] + term
            first = j * WIDE_PAD
            out_ref[:, first : first + head] = total[:, :head].astype(BF16)
            other = x_all[:, depth:].astype(F32) if j else jnp.zeros((total_rows, LANES), F32)
            out_ref[:, first + head : first + WIDE_PAD] = jnp.where(lane < SQUARES, total[:, head:], other).astype(BF16)

    return pl.pallas_call(
        kernel,
        in_specs=[IN_VMEM] * RING + [IN_HBM],
        out_specs=IN_VMEM,
        out_shape=jax.ShapeDtypeStruct((total_rows, 2 * WIDE_PAD), BF16),
        scratch_shapes=[
            pltpu.VMEM((pieces, WIDE, step), BF16),
            pltpu.VMEM((total_rows, width), BF16),
            pltpu.VMEM((total_rows, WIDE_PAD), F32),
            pltpu.SemaphoreType.DMA((pieces,)),
        ],
        compiler_params=pltpu.CompilerParams(vmem_limit_bytes=VMEM_BYTES),
        cost_estimate=pl.CostEstimate(
            flops=4 * total_rows * depth * WIDE, bytes_accessed=weights.size * 2, transcendentals=0
        ),
    )(*blocks, pltpu.with_memory_space_constraint(weights, pltpu.HBM))


def down_terms(act_ref, piece, out_refs):
    rows, width = out_refs[0].shape
    width //= RING
    for y in range(RING):
        w = piece(y)
        out = jnp.dot(act_ref[:, :UNITS], w[:UNITS], preferred_element_type=F32)
        out += jnp.dot(act_ref[:, ACT_PAD : ACT_PAD + UNITS], w[UNITS:], preferred_element_type=F32)
        for d in range(RING):
            out_refs[d][:, y * width : (y + 1) * width] = out[d * rows : (d + 1) * rows].astype(BF16)


def down_call(kernel, operands, lower, results, transcendentals):
    rows = operands[0].shape[0]
    width = lower.shape[1]
    shapes = results + [jax.ShapeDtypeStruct((rows // RING, RING * width), BF16)] * RING
    return pl.pallas_call(
        kernel,
        in_specs=[IN_VMEM] * len(operands) + [IN_HBM],
        out_specs=[IN_VMEM] * len(shapes),
        out_shape=shapes,
        scratch_shapes=[pltpu.VMEM((RING, 2 * UNITS, width), BF16), pltpu.SemaphoreType.DMA((RING,))],
        compiler_params=pltpu.CompilerParams(vmem_limit_bytes=VMEM_BYTES),
        cost_estimate=pl.CostEstimate(
            flops=2 * rows * lower.size, bytes_accessed=lower.size * 2, transcendentals=transcendentals
        ),
    )(*operands, pltpu.with_memory_space_constraint(lower, pltpu.HBM))


def activated_down(kept, got, lower):
    rows = kept.shape[0]

    def kernel(kept_ref, got_ref, w_ref, act_ref, *refs):
        out_refs, (held, sems) = refs[:RING], refs[RING:]
        piece = fetched(w_ref, held, sems)

        def both(first, columns):
            part = pl.ds(first, columns)
            return kept_ref[:, part].astype(F32) + got_ref[:, part].astype(F32)

        head = WIDE_PAD - LANES
        last = both(WIDE_PAD + head, LANES)
        lane = lax.broadcasted_iota(jnp.int32, last.shape, 1)
        carried = (lane >= SQUARES) & (lane < SQUARES + PIECES)
        squares = jnp.sum(jnp.where(carried, last, 0.0), axis=1, keepdims=True)
        scale = lax.rsqrt(squares / D + epsilon)

        def unit(gate, up):
            gate = gate * scale
            return gate / (1.0 + jnp.exp(-gate)) * (up * scale)

        for j in range(2):
            first, place = j * WIDE_PAD, j * ACT_PAD
            act_ref[:, place : place + MAIN] = unit(both(first, MAIN), both(first + MAIN, MAIN)).astype(BF16)
            tile = last if j else both(head, LANES)
            tails = unit(tile, pltpu.roll(tile, LANES - TAIL, 1))
            act_ref[:, place + MAIN : place + ACT_PAD] = jnp.where(lane < TAIL, tails, 0.0).astype(BF16)
        down_terms(act_ref, piece, out_refs)

    act, *out = down_call(
        kernel, [kept, got], lower, [jax.ShapeDtypeStruct((rows, 2 * ACT_PAD), BF16)], rows * WIDE
    )
    return act, out


def down_product(act, lower):
    def kernel(act_ref, w_ref, *refs):
        out_refs, (held, sems) = refs[:RING], refs[RING:]
        down_terms(act_ref, fetched(w_ref, held, sems), out_refs)

    return list(down_call(kernel, [act], lower, [], 0))


def block(column_give, keep, weights, lower, last):
    wide_give = from_behind(column_give, "x")
    if not last:
        (column_keep,) = after([keep()], *wide_give[1:])
        (wide_give[3],) = after([wide_give[3]], column_keep)
    given = partials(wide_give, weights)
    if last:
        (column_keep,) = after([keep()], given)
    wide_keep = from_behind(column_keep, "x")
    got = shifted(given, "z_lo", 1)
    kept = partials(wide_keep, weights)
    if not last:
        (lower,) = after([pltpu.with_memory_space_constraint(lower, pltpu.HBM)], kept[:16, :LANES])
    act_keep, out_keep = activated_down(kept, got, lower)
    act_give = shifted(act_keep, "z_lo", 1)
    got_keep = to_owners(out_keep, "x")
    out_give = down_product(act_give, lower)
    (got_keep[2],) = after([got_keep[2]], out_give[0])
    if not last:
        out_give[1:] = after(out_give[1:], got_keep[1], got_keep[3])
    got_give = to_owners(out_give, "x")
    return [sum(g.astype(F32) for g in got_keep), got_give]


def two_blocks(give, keep, gains, weights):
    column_keep, got_give = block(
        doubled(doubled(message(give, gains[0]), 1), 3),
        lambda: doubled(doubled(message(keep, gains[0]), 1), 3),
        *weights[0],
        False,
    )
    (keep,) = after([keep + halved(halved(column_keep, 3), 1)], *got_give[1:])
    rest = halved(sum(g.astype(F32) for g in got_give), 3)
    two = doubled(message(keep, gains[1]), 1)
    (rest,) = after([rest], two)
    column = doubled(two, 3)
    give = give + halved(rest, 1)
    column_give, got_keep = block(
        column, lambda: doubled(doubled(message(give, gains[1]), 1), 3), *weights[1], True
    )
    rest = halved(column_give, 3)
    (got_keep[2],) = after([got_keep[2]], rest)
    give = give + halved(rest, 1)
    keep = keep + halved(halved(sum(g.astype(F32) for g in got_keep), 3), 1)
    return give, keep


def stacked(gate, up, first):
    def kernel(first_ref, gate_ref, up_ref, out_ref):
        place = 0
        for skip, size in ((0, MAIN), (MAIN, TAIL)):
            for ref in (gate_ref, up_ref):
                out_ref[place : place + size, :] = ref[pl.ds(pl.multiple_of(first_ref[0] + skip, 16), size), :]
                place += size

    return pl.pallas_call(
        kernel,
        in_specs=[pl.BlockSpec(memory_space=pltpu.SMEM), IN_VMEM, IN_VMEM],
        out_specs=IN_VMEM,
        out_shape=jax.ShapeDtypeStruct((WIDE, gate.shape[1]), BF16),
        compiler_params=pltpu.CompilerParams(vmem_limit_bytes=VMEM_BYTES),
    )(first.astype(jnp.int32).reshape(1), gate, up)


def per_device(
    tokens,
    gain_first,
    gate_first,
    up_first,
    down_first,
    gain_second,
    gate_second,
    up_second,
    down_second,
):
    core, z_lo = lax.axis_index("section"), lax.axis_index("z_lo")
    width = tokens.shape[1]
    rows = tokens.shape[0] // RING
    part = rows // 2

    gains = jnp.concatenate([gain_first[None], gain_second[None], jnp.zeros((6, width), F32)], 0)
    leaving = jnp.concatenate(
        [tokens.reshape(RING, rows, width), jnp.broadcast_to(gains[None], (RING, *gains.shape))], 1
    )
    came = jnp.concatenate(jnp.split(lax.all_to_all(leaving, "y", 0, 0, tiled=True), RING, 0), 2)[0]
    keep = lax.dynamic_slice_in_dim(came, z_lo * part, part, 0)
    give = lax.dynamic_slice_in_dim(came, (1 - z_lo) * part, part, 0)

    def whole(upper, down):
        return (
            lax.all_gather(upper, ("section", "y"), axis=0, tiled=True),
            lax.all_gather(down, ("y", "section"), axis=0, tiled=True),
        )

    first = core * UNITS
    lower_first = lax.dynamic_slice_in_dim(down_first, first, UNITS, 0)
    weights_first = whole(stacked(gate_first.T, up_first.T, first), lower_first)
    weights_second = whole(stacked(gate_second.T, up_second.T, jnp.zeros_like(first)), down_second)

    gains = came[rows : rows + 1], came[rows + 1 : rows + 2]
    give, keep = two_blocks(give, keep, gains, (weights_first, weights_second))

    whole_rows = jnp.where(z_lo == 0, jnp.concatenate([keep, give], 0), jnp.concatenate([give, keep], 0))
    back = jnp.stack(jnp.split(whole_rows, RING, 1), 0)
    return lax.all_to_all(back, "y", 0, 0, tiled=True).reshape(tokens.shape)


def solution(mesh):
    axes = ("section", "x", "z_hi", "y", "z_lo")
    split = Mesh(mesh.devices.reshape(2, RING, RING, RING, 2), axes)
    hid, mod = ("x", "z_hi"), ("y", "z_lo")
    both = ("section", *hid)
    return jax.shard_map(
        per_device,
        mesh=split,
        in_specs=(
            P(both, mod),
            P(mod),
            P(mod, hid),
            P(mod, hid),
            P(hid, mod),
            P(mod),
            P(mod, both),
            P(mod, both),
            P(both, mod),
        ),
        out_specs=P(both, mod),
        check_vma=False,
    )
```

```python
import jax
import jax.numpy as jnp
from jax import lax
from jax.experimental import pallas as pl
from jax.experimental.pallas import tpu as pltpu
from jax.sharding import Mesh
from jax.sharding import PartitionSpec as P

D = 5120
RING = 4
AHEAD = (2, 1, 3)
LANES = 128
epsilon = 1e-06
BF16 = jnp.bfloat16
F32 = jnp.float32

MAIN, TAIL = 384, 48
UNITS = MAIN + TAIL
WIDE = 2 * UNITS
WIDE_PAD = 896
ACT_PAD = 512
SQUARES = 2 * TAIL
PIECES = 3
VMEM_BYTES = 24 * 1024 * 1024


def shifted(x, axis, distance):
    size = lax.axis_size(axis)
    return lax.ppermute(x, axis, [(i, (i + distance) % size) for i in range(size)])


def after(xs, *others):
    anywhere = pl.BlockSpec(memory_space=pl.ANY)
    return pl.pallas_call(
        lambda *refs: None,
        out_shape=[jax.ShapeDtypeStruct(x.shape, x.dtype) for x in xs],
        in_specs=[anywhere] * (len(xs) + len(others)),
        out_specs=[anywhere] * len(xs),
        input_output_aliases={i: i for i in range(len(xs))},
    )(*xs, *others)


def from_behind(x, axis):
    got = {d: shifted(x, axis, d) for d in AHEAD}
    return [x, got[1], got[2], got[3]]


def to_owners(blocks, axis):
    return [blocks[0]] + [shifted(blocks[d], axis, -d) for d in AHEAD]


def paired(x, axis, flip):
    return lax.ppermute(x, axis, [(i, i ^ flip) for i in range(RING)])


def doubled(x, flip):
    return jnp.concatenate([x, paired(x, "z_hi", flip)], 0)


def halved(x, flip):
    half = x.shape[0] // 2
    return x[:half] + paired(x[half:].astype(BF16), "z_hi", flip).astype(F32)


def three_pieces(x):
    high = lax.reduce_precision(x, 8, 7)
    middle = lax.reduce_precision(x - high, 8, 7)
    low = x - high - middle
    return [high.astype(BF16), middle.astype(BF16), low.astype(BF16)]


def message(v, gain):
    squares = jnp.sum(v * v, axis=1, keepdims=True)
    pieces = three_pieces(squares)
    blank = jnp.zeros((v.shape[0], LANES), BF16)
    return jnp.concatenate(
        [(v * gain).astype(BF16), blank[:, :SQUARES], *pieces, blank[:, : LANES - SQUARES - PIECES]], 1
    )


IN_VMEM = pl.BlockSpec(memory_space=pltpu.VMEM)
IN_HBM = pl.BlockSpec(memory_space=pltpu.HBM)


def fetched(w_ref, held, sems):
    pieces, size, _ = held.shape
    copies = [
        pltpu.make_async_copy(w_ref.at[pl.ds(i * size, size)], held.at[i], sems.at[i]) for i in range(pieces)
    ]
    for copy in copies:
        copy.start()

    def wait(i):
        copies[i].wait()
        return held[i]

    return wait


def partials(blocks, weights):
    rows, width = blocks[0].shape
    total_rows = RING * rows
    step = weights.shape[1]
    depth = RING * step
    pieces = 2 * RING

    def kernel(*refs):
        x_refs, (w_ref, out_ref, held, x_all, total, sems) = refs[:RING], refs[RING:]
        piece = fetched(w_ref, held, sems)
        for d in range(RING):
            x_all[d * rows : (d + 1) * rows, :] = x_refs[d][...]
        lane = lax.broadcasted_iota(jnp.int32, (total_rows, LANES), 1)
        head = WIDE_PAD - LANES
        for j in range(2):
            for y in range(RING):
                term = lax.dot_general(
                    x_all[:, y * step : (y + 1) * step],
                    piece(j * RING + y),
                    (((1,), (1,)), ((), ())),
                    preferred_element_type=F32,
                )
                total[:, :WIDE] = term if y == 0 else total[:, :WIDE] + term
            first = j * WIDE_PAD
            out_ref[:, first : first + head] = total[:, :head].astype(BF16)
            other = x_all[:, depth:].astype(F32) if j else jnp.zeros((total_rows, LANES), F32)
            out_ref[:, first + head : first + WIDE_PAD] = jnp.where(lane < SQUARES, total[:, head:], other).astype(BF16)

    return pl.pallas_call(
        kernel,
        in_specs=[IN_VMEM] * RING + [IN_HBM],
        out_specs=IN_VMEM,
        out_shape=jax.ShapeDtypeStruct((total_rows, 2 * WIDE_PAD), BF16),
        scratch_shapes=[
            pltpu.VMEM((pieces, WIDE, step), BF16),
            pltpu.VMEM((total_rows, width), BF16),
            pltpu.VMEM((total_rows, WIDE_PAD), F32),
            pltpu.SemaphoreType.DMA((pieces,)),
        ],
        compiler_params=pltpu.CompilerParams(vmem_limit_bytes=VMEM_BYTES),
        cost_estimate=pl.CostEstimate(
            flops=4 * total_rows * depth * WIDE, bytes_accessed=weights.size * 2, transcendentals=0
        ),
    )(*blocks, pltpu.with_memory_space_constraint(weights, pltpu.HBM))


def down_terms(act_ref, piece, out_refs):
    rows, width = out_refs[0].shape
    width //= RING
    for y in range(RING):
        w = piece(y)
        out = jnp.dot(act_ref[:, :UNITS], w[:UNITS], preferred_element_type=F32)
        out += jnp.dot(act_ref[:, ACT_PAD : ACT_PAD + UNITS], w[UNITS:], preferred_element_type=F32)
        for d in range(RING):
            out_refs[d][:, y * width : (y + 1) * width] = out[d * rows : (d + 1) * rows].astype(BF16)


def down_call(kernel, operands, lower, results, transcendentals):
    rows = operands[0].shape[0]
    width = lower.shape[1]
    shapes = results + [jax.ShapeDtypeStruct((rows // RING, RING * width), BF16)] * RING
    return pl.pallas_call(
        kernel,
        in_specs=[IN_VMEM] * len(operands) + [IN_HBM],
        out_specs=[IN_VMEM] * len(shapes),
        out_shape=shapes,
        scratch_shapes=[pltpu.VMEM((RING, 2 * UNITS, width), BF16), pltpu.SemaphoreType.DMA((RING,))],
        compiler_params=pltpu.CompilerParams(vmem_limit_bytes=VMEM_BYTES),
        cost_estimate=pl.CostEstimate(
            flops=2 * rows * lower.size, bytes_accessed=lower.size * 2, transcendentals=transcendentals
        ),
    )(*operands, pltpu.with_memory_space_constraint(lower, pltpu.HBM))


def activated_down(kept, got, lower):
    rows = kept.shape[0]

    def kernel(kept_ref, got_ref, w_ref, act_ref, *refs):
        out_refs, (held, sems) = refs[:RING], refs[RING:]
        piece = fetched(w_ref, held, sems)

        def both(first, columns):
            part = pl.ds(first, columns)
            return kept_ref[:, part].astype(F32) + got_ref[:, part].astype(F32)

        head = WIDE_PAD - LANES
        last = both(WIDE_PAD + head, LANES)
        lane = lax.broadcasted_iota(jnp.int32, last.shape, 1)
        carried = (lane >= SQUARES) & (lane < SQUARES + PIECES)
        squares = jnp.sum(jnp.where(carried, last, 0.0), axis=1, keepdims=True)
        scale = lax.rsqrt(squares / D + epsilon)

        def unit(gate, up):
            gate = gate * scale
            return gate / (1.0 + jnp.exp(-gate)) * (up * scale)

        for j in range(2):
            first, place = j * WIDE_PAD, j * ACT_PAD
            act_ref[:, place : place + MAIN] = unit(both(first, MAIN), both(first + MAIN, MAIN)).astype(BF16)
            tile = last if j else both(head, LANES)
            tails = unit(tile, pltpu.roll(tile, LANES - TAIL, 1))
            act_ref[:, place + MAIN : place + ACT_PAD] = jnp.where(lane < TAIL, tails, 0.0).astype(BF16)
        down_terms(act_ref, piece, out_refs)

    act, *out = down_call(
        kernel, [kept, got], lower, [jax.ShapeDtypeStruct((rows, 2 * ACT_PAD), BF16)], rows * WIDE
    )
    return act, out


def down_product(act, lower):
    def kernel(act_ref, w_ref, *refs):
        out_refs, (held, sems) = refs[:RING], refs[RING:]
        down_terms(act_ref, fetched(w_ref, held, sems), out_refs)

    return list(down_call(kernel, [act], lower, [], 0))


def block(column_give, keep, weights, lower, last):
    wide_give = from_behind(column_give, "x")
    given = partials(wide_give, weights)
    (column_keep,) = after([keep()], *([given] if last else wide_give[1:]))
    wide_keep = from_behind(column_keep, "x")
    got = shifted(given, "z_lo", 1)
    kept = partials(wide_keep, weights)
    if not last:
        (lower,) = after([pltpu.with_memory_space_constraint(lower, pltpu.HBM)], kept[:16, :LANES])
    act_keep, out_keep = activated_down(kept, got, lower)
    act_give = shifted(act_keep, "z_lo", 1)
    got_keep = to_owners(out_keep, "x")
    out_give = down_product(act_give, lower)
    (got_keep[2],) = after([got_keep[2]], out_give[0])
    got_give = to_owners(out_give, "x")
    return [sum(g.astype(F32) for g in got_keep), got_give]


def two_blocks(give, keep, gains, weights):
    column_keep, got_give = block(
        doubled(doubled(message(give, gains[0]), 1), 3),
        lambda: doubled(doubled(message(keep, gains[0]), 1), 3),
        *weights[0],
        False,
    )
    (rest,) = after([halved(column_keep, 3)], *got_give[1:])
    keep = keep + halved(rest, 1)
    rest = halved(sum(g.astype(F32) for g in got_give), 3)
    two = doubled(message(keep, gains[1]), 1)
    (rest,) = after([rest], two)
    column = doubled(two, 3)
    give = give + halved(rest, 1)
    column_give, got_keep = block(
        column, lambda: doubled(doubled(message(give, gains[1]), 1), 3), *weights[1], True
    )
    give = give + halved(halved(column_give, 3), 1)
    keep = keep + halved(halved(sum(g.astype(F32) for g in got_keep), 3), 1)
    return give, keep


def stacked(gate, up, first):
    def kernel(first_ref, gate_ref, up_ref, out_ref):
        place = 0
        for skip, size in ((0, MAIN), (MAIN, TAIL)):
            for ref in (gate_ref, up_ref):
                out_ref[place : place + size, :] = ref[pl.ds(pl.multiple_of(first_ref[0] + skip, 16), size), :]
                place += size

    return pl.pallas_call(
        kernel,
        in_specs=[pl.BlockSpec(memory_space=pltpu.SMEM), IN_VMEM, IN_VMEM],
        out_specs=IN_VMEM,
        out_shape=jax.ShapeDtypeStruct((WIDE, gate.shape[1]), BF16),
        compiler_params=pltpu.CompilerParams(vmem_limit_bytes=VMEM_BYTES),
    )(first.astype(jnp.int32).reshape(1), gate, up)


def per_device(
    tokens,
    gain_first,
    gate_first,
    up_first,
    down_first,
    gain_second,
    gate_second,
    up_second,
    down_second,
):
    core, z_lo = lax.axis_index("section"), lax.axis_index("z_lo")
    width = tokens.shape[1]
    rows = tokens.shape[0] // RING
    part = rows // 2

    gains = jnp.concatenate([gain_first[None], gain_second[None], jnp.zeros((6, width), F32)], 0)
    leaving = jnp.concatenate(
        [tokens.reshape(RING, rows, width), jnp.broadcast_to(gains[None], (RING, *gains.shape))], 1
    )
    came = jnp.concatenate(jnp.split(lax.all_to_all(leaving, "y", 0, 0, tiled=True), RING, 0), 2)[0]
    keep = lax.dynamic_slice_in_dim(came, z_lo * part, part, 0)
    give = lax.dynamic_slice_in_dim(came, (1 - z_lo) * part, part, 0)

    def whole(upper, down):
        return (
            lax.all_gather(upper, ("section", "y"), axis=0, tiled=True),
            lax.all_gather(down, ("y", "section"), axis=0, tiled=True),
        )

    first = core * UNITS
    lower_first = lax.dynamic_slice_in_dim(down_first, first, UNITS, 0)
    weights_first = whole(stacked(gate_first.T, up_first.T, first), lower_first)
    weights_second = whole(stacked(gate_second.T, up_second.T, jnp.zeros_like(first)), down_second)

    gains = came[rows : rows + 1], came[rows + 1 : rows + 2]
    give, keep = two_blocks(give, keep, gains, (weights_first, weights_second))

    whole_rows = jnp.where(z_lo == 0, jnp.concatenate([keep, give], 0), jnp.concatenate([give, keep], 0))
    back = jnp.stack(jnp.split(whole_rows, RING, 1), 0)
    return lax.all_to_all(back, "y", 0, 0, tiled=True).reshape(tokens.shape)


def solution(mesh):
    axes = ("section", "x", "z_hi", "y", "z_lo")
    split = Mesh(mesh.devices.reshape(2, RING, RING, RING, 2), axes)
    hid, mod = ("x", "z_hi"), ("y", "z_lo")
    both = ("section", *hid)
    return jax.shard_map(
        per_device,
        mesh=split,
        in_specs=(
            P(both, mod),
            P(mod),
            P(mod, hid),
            P(mod, hid),
            P(hid, mod),
            P(mod),
            P(mod, both),
            P(mod, both),
            P(both, mod),
        ),
        out_specs=P(both, mod),
        check_vma=False,
    )
```

```python
import jax
import jax.numpy as jnp
from jax import lax
from jax.experimental import pallas as pl
from jax.experimental.pallas import tpu as pltpu
from jax.sharding import Mesh
from jax.sharding import PartitionSpec as P

D = 5120
RING = 4
AHEAD = (2, 1, 3)
LANES = 128
epsilon = 1e-06
BF16 = jnp.bfloat16
F32 = jnp.float32

MAIN, TAIL = 384, 48
UNITS = MAIN + TAIL
WIDE = 2 * UNITS
WIDE_PAD = 896
ACT_PAD = 512
SQUARES = 2 * TAIL
PIECES = 3
VMEM_BYTES = 24 * 1024 * 1024


def shifted(x, axis, distance):
    size = lax.axis_size(axis)
    return lax.ppermute(x, axis, [(i, (i + distance) % size) for i in range(size)])


def after(xs, *others):
    anywhere = pl.BlockSpec(memory_space=pl.ANY)
    return pl.pallas_call(
        lambda *refs: None,
        out_shape=[jax.ShapeDtypeStruct(x.shape, x.dtype) for x in xs],
        in_specs=[anywhere] * (len(xs) + len(others)),
        out_specs=[anywhere] * len(xs),
        input_output_aliases={i: i for i in range(len(xs))},
    )(*xs, *others)


def from_behind(x, axis):
    got = {d: shifted(x, axis, d) for d in AHEAD}
    return [x, got[1], got[2], got[3]]


def to_owners(blocks, axis):
    return [blocks[0]] + [shifted(blocks[d], axis, -d) for d in AHEAD]


def paired(x, axis, flip):
    return lax.ppermute(x, axis, [(i, i ^ flip) for i in range(RING)])


def doubled(x, flip):
    return jnp.concatenate([x, paired(x, "z_hi", flip)], 0)


def halved(x, flip, *others):
    half = x.shape[0] // 2
    here = x[:half]
    if others:
        (here,) = after([here], *others)
    return here + paired(x[half:].astype(BF16), "z_hi", flip).astype(F32)


def three_pieces(x):
    high = lax.reduce_precision(x, 8, 7)
    middle = lax.reduce_precision(x - high, 8, 7)
    low = x - high - middle
    return [high.astype(BF16), middle.astype(BF16), low.astype(BF16)]


def message(v, gain):
    squares = jnp.sum(v * v, axis=1, keepdims=True)
    pieces = three_pieces(squares)
    blank = jnp.zeros((v.shape[0], LANES), BF16)
    return jnp.concatenate(
        [(v * gain).astype(BF16), blank[:, :SQUARES], *pieces, blank[:, : LANES - SQUARES - PIECES]], 1
    )


IN_VMEM = pl.BlockSpec(memory_space=pltpu.VMEM)
IN_HBM = pl.BlockSpec(memory_space=pltpu.HBM)


def fetched(w_ref, held, sems):
    pieces, size, _ = held.shape
    copies = [
        pltpu.make_async_copy(w_ref.at[pl.ds(i * size, size)], held.at[i], sems.at[i]) for i in range(pieces)
    ]
    for copy in copies:
        copy.start()

    def wait(i):
        copies[i].wait()
        return held[i]

    return wait


def partials(blocks, weights):
    rows, width = blocks[0].shape
    total_rows = RING * rows
    step = weights.shape[1]
    depth = RING * step
    pieces = 2 * RING

    def kernel(*refs):
        x_refs, (w_ref, out_ref, held, x_all, total, sems) = refs[:RING], refs[RING:]
        piece = fetched(w_ref, held, sems)
        for d in range(RING):
            x_all[d * rows : (d + 1) * rows, :] = x_refs[d][...]
        lane = lax.broadcasted_iota(jnp.int32, (total_rows, LANES), 1)
        head = WIDE_PAD - LANES
        for j in range(2):
            for y in range(RING):
                term = lax.dot_general(
                    x_all[:, y * step : (y + 1) * step],
                    piece(j * RING + y),
                    (((1,), (1,)), ((), ())),
                    preferred_element_type=F32,
                )
                total[:, :WIDE] = term if y == 0 else total[:, :WIDE] + term
            first = j * WIDE_PAD
            out_ref[:, first : first + head] = total[:, :head].astype(BF16)
            other = x_all[:, depth:].astype(F32) if j else jnp.zeros((total_rows, LANES), F32)
            out_ref[:, first + head : first + WIDE_PAD] = jnp.where(lane < SQUARES, total[:, head:], other).astype(BF16)

    return pl.pallas_call(
        kernel,
        in_specs=[IN_VMEM] * RING + [IN_HBM],
        out_specs=IN_VMEM,
        out_shape=jax.ShapeDtypeStruct((total_rows, 2 * WIDE_PAD), BF16),
        scratch_shapes=[
            pltpu.VMEM((pieces, WIDE, step), BF16),
            pltpu.VMEM((total_rows, width), BF16),
            pltpu.VMEM((total_rows, WIDE_PAD), F32),
            pltpu.SemaphoreType.DMA((pieces,)),
        ],
        compiler_params=pltpu.CompilerParams(vmem_limit_bytes=VMEM_BYTES),
        cost_estimate=pl.CostEstimate(
            flops=4 * total_rows * depth * WIDE, bytes_accessed=weights.size * 2, transcendentals=0
        ),
    )(*blocks, pltpu.with_memory_space_constraint(weights, pltpu.HBM))


def down_terms(act_ref, piece, out_refs):
    rows, width = out_refs[0].shape
    width //= RING
    for y in range(RING):
        w = piece(y)
        out = jnp.dot(act_ref[:, :UNITS], w[:UNITS], preferred_element_type=F32)
        out += jnp.dot(act_ref[:, ACT_PAD : ACT_PAD + UNITS], w[UNITS:], preferred_element_type=F32)
        for d in range(RING):
            out_refs[d][:, y * width : (y + 1) * width] = out[d * rows : (d + 1) * rows].astype(BF16)


def down_call(kernel, operands, lower, results, transcendentals):
    rows = operands[0].shape[0]
    width = lower.shape[1]
    shapes = results + [jax.ShapeDtypeStruct((rows // RING, RING * width), BF16)] * RING
    return pl.pallas_call(
        kernel,
        in_specs=[IN_VMEM] * len(operands) + [IN_HBM],
        out_specs=[IN_VMEM] * len(shapes),
        out_shape=shapes,
        scratch_shapes=[pltpu.VMEM((RING, 2 * UNITS, width), BF16), pltpu.SemaphoreType.DMA((RING,))],
        compiler_params=pltpu.CompilerParams(vmem_limit_bytes=VMEM_BYTES),
        cost_estimate=pl.CostEstimate(
            flops=2 * rows * lower.size, bytes_accessed=lower.size * 2, transcendentals=transcendentals
        ),
    )(*operands, pltpu.with_memory_space_constraint(lower, pltpu.HBM))


def activated_down(kept, got, lower):
    rows = kept.shape[0]

    def kernel(kept_ref, got_ref, w_ref, act_ref, *refs):
        out_refs, (held, sems) = refs[:RING], refs[RING:]
        piece = fetched(w_ref, held, sems)

        def both(first, columns):
            part = pl.ds(first, columns)
            return kept_ref[:, part].astype(F32) + got_ref[:, part].astype(F32)

        head = WIDE_PAD - LANES
        last = both(WIDE_PAD + head, LANES)
        lane = lax.broadcasted_iota(jnp.int32, last.shape, 1)
        carried = (lane >= SQUARES) & (lane < SQUARES + PIECES)
        squares = jnp.sum(jnp.where(carried, last, 0.0), axis=1, keepdims=True)
        scale = lax.rsqrt(squares / D + epsilon)

        def unit(gate, up):
            gate = gate * scale
            return gate / (1.0 + jnp.exp(-gate)) * (up * scale)

        for j in range(2):
            first, place = j * WIDE_PAD, j * ACT_PAD
            act_ref[:, place : place + MAIN] = unit(both(first, MAIN), both(first + MAIN, MAIN)).astype(BF16)
            tile = last if j else both(head, LANES)
            tails = unit(tile, pltpu.roll(tile, LANES - TAIL, 1))
            act_ref[:, place + MAIN : place + ACT_PAD] = jnp.where(lane < TAIL, tails, 0.0).astype(BF16)
        down_terms(act_ref, piece, out_refs)

    act, *out = down_call(
        kernel, [kept, got], lower, [jax.ShapeDtypeStruct((rows, 2 * ACT_PAD), BF16)], rows * WIDE
    )
    return act, out


def down_product(act, lower):
    def kernel(act_ref, w_ref, *refs):
        out_refs, (held, sems) = refs[:RING], refs[RING:]
        down_terms(act_ref, fetched(w_ref, held, sems), out_refs)

    return list(down_call(kernel, [act], lower, [], 0))


def block(column_give, keep, weights, lower, last):
    wide_give = from_behind(column_give, "x")
    given = partials(wide_give, weights)
    (column_keep,) = after([keep()], *([given] if last else wide_give[1:]))
    wide_keep = from_behind(column_keep, "x")
    got = shifted(given, "z_lo", 1)
    kept = partials(wide_keep, weights)
    if not last:
        (lower,) = after([pltpu.with_memory_space_constraint(lower, pltpu.HBM)], kept[:16, :LANES])
    act_keep, out_keep = activated_down(kept, got, lower)
    act_give = shifted(act_keep, "z_lo", 1)
    got_keep = to_owners(out_keep, "x")
    out_give = down_product(act_give, lower)
    (got_keep[2],) = after([got_keep[2]], out_give[0])
    got_give = to_owners(out_give, "x")
    return [sum(g.astype(F32) for g in got_keep), got_give]


def two_blocks(give, keep, gains, weights):
    column_keep, got_give = block(
        doubled(doubled(message(give, gains[0]), 1), 3),
        lambda: doubled(doubled(message(keep, gains[0]), 1), 3),
        *weights[0],
        False,
    )
    keep = keep + halved(halved(column_keep, 3, *got_give[1:]), 1)
    rest = halved(sum(g.astype(F32) for g in got_give), 3)
    two = doubled(message(keep, gains[1]), 1)
    (rest,) = after([rest], two)
    column = doubled(two, 3)
    give = give + halved(rest, 1)
    column_give, got_keep = block(
        column, lambda: doubled(doubled(message(give, gains[1]), 1), 3), *weights[1], True
    )
    give = give + halved(halved(column_give, 3), 1)
    keep = keep + halved(halved(sum(g.astype(F32) for g in got_keep), 3), 1)
    return give, keep


def stacked(gate, up, first):
    def kernel(first_ref, gate_ref, up_ref, out_ref, sems):
        copies = []
        place = 0
        for skip, size in ((0, MAIN), (MAIN, TAIL)):
            for ref in (gate_ref, up_ref):
                rows = pl.ds(pl.multiple_of(first_ref[0] + skip, 16), size)
                copies.append(
                    pltpu.make_async_copy(ref.at[rows], out_ref.at[pl.ds(place, size)], sems.at[len(copies)])
                )
                place += size
        for copy in copies:
            copy.start()
        for copy in copies:
            copy.wait()

    return pl.pallas_call(
        kernel,
        in_specs=[pl.BlockSpec(memory_space=pltpu.SMEM), IN_HBM, IN_HBM],
        out_specs=IN_VMEM,
        out_shape=jax.ShapeDtypeStruct((WIDE, gate.shape[1]), BF16),
        scratch_shapes=[pltpu.SemaphoreType.DMA((4,))],
        compiler_params=pltpu.CompilerParams(vmem_limit_bytes=VMEM_BYTES),
    )(
        first.astype(jnp.int32).reshape(1),
        *(pltpu.with_memory_space_constraint(w, pltpu.HBM) for w in (gate, up)),
    )


def per_device(
    tokens,
    gain_first,
    gate_first,
    up_first,
    down_first,
    gain_second,
    gate_second,
    up_second,
    down_second,
):
    core, z_lo = lax.axis_index("section"), lax.axis_index("z_lo")
    width = tokens.shape[1]
    rows = tokens.shape[0] // RING
    part = rows // 2

    gains = jnp.concatenate([gain_first[None], gain_second[None], jnp.zeros((6, width), F32)], 0)
    leaving = jnp.concatenate(
        [tokens.reshape(RING, rows, width), jnp.broadcast_to(gains[None], (RING, *gains.shape))], 1
    )
    came = jnp.concatenate(jnp.split(lax.all_to_all(leaving, "y", 0, 0, tiled=True), RING, 0), 2)[0]
    keep = lax.dynamic_slice_in_dim(came, z_lo * part, part, 0)
    give = lax.dynamic_slice_in_dim(came, (1 - z_lo) * part, part, 0)

    def whole(upper, down):
        return (
            lax.all_gather(upper, ("section", "y"), axis=0, tiled=True),
            lax.all_gather(down, ("y", "section"), axis=0, tiled=True),
        )

    first = core * UNITS
    lower_first = lax.dynamic_slice_in_dim(down_first, first, UNITS, 0)
    weights_first = whole(stacked(gate_first.T, up_first.T, first), lower_first)
    weights_second = whole(stacked(gate_second.T, up_second.T, jnp.zeros_like(first)), down_second)

    gains = came[rows : rows + 1], came[rows + 1 : rows + 2]
    give, keep = two_blocks(give, keep, gains, (weights_first, weights_second))

    whole_rows = jnp.where(z_lo == 0, jnp.concatenate([keep, give], 0), jnp.concatenate([give, keep], 0))
    back = jnp.stack(jnp.split(whole_rows, RING, 1), 0)
    return lax.all_to_all(back, "y", 0, 0, tiled=True).reshape(tokens.shape)


def solution(mesh):
    axes = ("section", "x", "z_hi", "y", "z_lo")
    split = Mesh(mesh.devices.reshape(2, RING, RING, RING, 2), axes)
    hid, mod = ("x", "z_hi"), ("y", "z_lo")
    both = ("section", *hid)
    return jax.shard_map(
        per_device,
        mesh=split,
        in_specs=(
            P(both, mod),
            P(mod),
            P(mod, hid),
            P(mod, hid),
            P(hid, mod),
            P(mod),
            P(mod, both),
            P(mod, both),
            P(both, mod),
        ),
        out_specs=P(both, mod),
        check_vma=False,
    )
```

```python
import jax
import jax.numpy as jnp
from jax import lax
from jax.experimental import pallas as pl
from jax.experimental.pallas import tpu as pltpu
from jax.sharding import Mesh
from jax.sharding import PartitionSpec as P

D = 5120
RING = 4
AHEAD = (2, 1, 3)
LANES = 128
epsilon = 1e-06
BF16 = jnp.bfloat16
F32 = jnp.float32

MAIN, TAIL = 384, 48
UNITS = MAIN + TAIL
WIDE = 2 * UNITS
WIDE_PAD = 896
ACT_PAD = 512
SQUARES = 2 * TAIL
PIECES = 3
VMEM_BYTES = 24 * 1024 * 1024


def shifted(x, axis, distance):
    size = lax.axis_size(axis)
    return lax.ppermute(x, axis, [(i, (i + distance) % size) for i in range(size)])


def after(xs, *others):
    anywhere = pl.BlockSpec(memory_space=pl.ANY)
    return pl.pallas_call(
        lambda *refs: None,
        out_shape=[jax.ShapeDtypeStruct(x.shape, x.dtype) for x in xs],
        in_specs=[anywhere] * (len(xs) + len(others)),
        out_specs=[anywhere] * len(xs),
        input_output_aliases={i: i for i in range(len(xs))},
    )(*xs, *others)


def from_behind(x, axis):
    got = {d: shifted(x, axis, d) for d in AHEAD}
    return [x, got[1], got[2], got[3]]


def to_owners(blocks, axis):
    return [blocks[0]] + [shifted(blocks[d], axis, -d) for d in AHEAD]


def paired(x, axis, flip):
    return lax.ppermute(x, axis, [(i, i ^ flip) for i in range(RING)])


def doubled(x, flip):
    return jnp.concatenate([x, paired(x, "z_hi", flip)], 0)


def halved(x, flip, *others):
    half = x.shape[0] // 2
    here = x[:half]
    if others:
        (here,) = after([here], *others)
    return here + paired(x[half:].astype(BF16), "z_hi", flip).astype(F32)


def three_pieces(x):
    high = lax.reduce_precision(x, 8, 7)
    middle = lax.reduce_precision(x - high, 8, 7)
    low = x - high - middle
    return [high.astype(BF16), middle.astype(BF16), low.astype(BF16)]


def message(v, gain):
    squares = jnp.sum(v * v, axis=1, keepdims=True)
    pieces = three_pieces(squares)
    blank = jnp.zeros((v.shape[0], LANES), BF16)
    return jnp.concatenate(
        [(v * gain).astype(BF16), blank[:, :SQUARES], *pieces, blank[:, : LANES - SQUARES - PIECES]], 1
    )


IN_VMEM = pl.BlockSpec(memory_space=pltpu.VMEM)
IN_HBM = pl.BlockSpec(memory_space=pltpu.HBM)


def fetched(w_ref, held, sems):
    pieces, size, _ = held.shape
    copies = [
        pltpu.make_async_copy(w_ref.at[pl.ds(i * size, size)], held.at[i], sems.at[i]) for i in range(pieces)
    ]
    for copy in copies:
        copy.start()

    def wait(i):
        copies[i].wait()
        return held[i]

    return wait


def partials(blocks, weights):
    rows, width = blocks[0].shape
    total_rows = RING * rows
    step = weights.shape[1]
    depth = RING * step
    pieces = 2 * RING

    def kernel(*refs):
        x_refs, (w_ref, out_ref, held, x_all, total, sems) = refs[:RING], refs[RING:]
        piece = fetched(w_ref, held, sems)
        for d in range(RING):
            x_all[d * rows : (d + 1) * rows, :] = x_refs[d][...]
        lane = lax.broadcasted_iota(jnp.int32, (total_rows, LANES), 1)
        head = WIDE_PAD - LANES
        for j in range(2):
            for y in range(RING):
                term = lax.dot_general(
                    x_all[:, y * step : (y + 1) * step],
                    piece(j * RING + y),
                    (((1,), (1,)), ((), ())),
                    preferred_element_type=F32,
                )
                total[:, :WIDE] = term if y == 0 else total[:, :WIDE] + term
            first = j * WIDE_PAD
            out_ref[:, first : first + head] = total[:, :head].astype(BF16)
            other = x_all[:, depth:].astype(F32) if j else jnp.zeros((total_rows, LANES), F32)
            out_ref[:, first + head : first + WIDE_PAD] = jnp.where(lane < SQUARES, total[:, head:], other).astype(BF16)

    return pl.pallas_call(
        kernel,
        in_specs=[IN_VMEM] * RING + [IN_HBM],
        out_specs=IN_VMEM,
        out_shape=jax.ShapeDtypeStruct((total_rows, 2 * WIDE_PAD), BF16),
        scratch_shapes=[
            pltpu.VMEM((pieces, WIDE, step), BF16),
            pltpu.VMEM((total_rows, width), BF16),
            pltpu.VMEM((total_rows, WIDE_PAD), F32),
            pltpu.SemaphoreType.DMA((pieces,)),
        ],
        compiler_params=pltpu.CompilerParams(vmem_limit_bytes=VMEM_BYTES),
        cost_estimate=pl.CostEstimate(
            flops=4 * total_rows * depth * WIDE, bytes_accessed=weights.size * 2, transcendentals=0
        ),
    )(*blocks, pltpu.with_memory_space_constraint(weights, pltpu.HBM))


def down_terms(act_ref, piece, out_refs):
    rows, width = out_refs[0].shape
    width //= RING
    for y in range(RING):
        w = piece(y)
        out = jnp.dot(act_ref[:, :UNITS], w[:UNITS], preferred_element_type=F32)
        out += jnp.dot(act_ref[:, ACT_PAD : ACT_PAD + UNITS], w[UNITS:], preferred_element_type=F32)
        for d in range(RING):
            out_refs[d][:, y * width : (y + 1) * width] = out[d * rows : (d + 1) * rows].astype(BF16)


def down_call(kernel, operands, lower, results, transcendentals):
    rows = operands[0].shape[0]
    width = lower.shape[1]
    shapes = results + [jax.ShapeDtypeStruct((rows // RING, RING * width), BF16)] * RING
    return pl.pallas_call(
        kernel,
        in_specs=[IN_VMEM] * len(operands) + [IN_HBM],
        out_specs=[IN_VMEM] * len(shapes),
        out_shape=shapes,
        scratch_shapes=[pltpu.VMEM((RING, 2 * UNITS, width), BF16), pltpu.SemaphoreType.DMA((RING,))],
        compiler_params=pltpu.CompilerParams(vmem_limit_bytes=VMEM_BYTES),
        cost_estimate=pl.CostEstimate(
            flops=2 * rows * lower.size, bytes_accessed=lower.size * 2, transcendentals=transcendentals
        ),
    )(*operands, pltpu.with_memory_space_constraint(lower, pltpu.HBM))


def activated_down(kept, got, lower):
    rows = kept.shape[0]

    def kernel(kept_ref, got_ref, w_ref, act_ref, *refs):
        out_refs, (held, sems) = refs[:RING], refs[RING:]
        piece = fetched(w_ref, held, sems)

        def both(first, columns):
            part = pl.ds(first, columns)
            return kept_ref[:, part].astype(F32) + got_ref[:, part].astype(F32)

        head = WIDE_PAD - LANES
        last = both(WIDE_PAD + head, LANES)
        lane = lax.broadcasted_iota(jnp.int32, last.shape, 1)
        carried = (lane >= SQUARES) & (lane < SQUARES + PIECES)
        squares = jnp.sum(jnp.where(carried, last, 0.0), axis=1, keepdims=True)
        scale = lax.rsqrt(squares / D + epsilon)

        def unit(gate, up):
            gate = gate * scale
            return gate / (1.0 + jnp.exp(-gate)) * (up * scale)

        for j in range(2):
            first, place = j * WIDE_PAD, j * ACT_PAD
            act_ref[:, place : place + MAIN] = unit(both(first, MAIN), both(first + MAIN, MAIN)).astype(BF16)
            tile = last if j else both(head, LANES)
            tails = unit(tile, pltpu.roll(tile, LANES - TAIL, 1))
            act_ref[:, place + MAIN : place + ACT_PAD] = jnp.where(lane < TAIL, tails, 0.0).astype(BF16)
        down_terms(act_ref, piece, out_refs)

    act, *out = down_call(
        kernel, [kept, got], lower, [jax.ShapeDtypeStruct((rows, 2 * ACT_PAD), BF16)], rows * WIDE
    )
    return act, out


def down_product(act, lower):
    def kernel(act_ref, w_ref, *refs):
        out_refs, (held, sems) = refs[:RING], refs[RING:]
        down_terms(act_ref, fetched(w_ref, held, sems), out_refs)

    return list(down_call(kernel, [act], lower, [], 0))


def block(column_give, keep, weights, lower, last):
    wide_give = from_behind(column_give, "x")
    given = partials(wide_give, weights)
    (column_keep,) = after([keep()], *([given] if last else wide_give[1:]))
    wide_keep = from_behind(column_keep, "x")
    got = shifted(given, "z_lo", 1)
    kept = partials(wide_keep, weights)
    if not last:
        (lower,) = after([pltpu.with_memory_space_constraint(lower, pltpu.HBM)], kept[:16, :LANES])
    act_keep, out_keep = activated_down(kept, got, lower)
    act_give = shifted(act_keep, "z_lo", 1)
    got_keep = to_owners(out_keep, "x")
    out_give = down_product(act_give, lower)
    (got_keep[2],) = after([got_keep[2]], out_give[0])
    got_give = to_owners(out_give, "x")
    return [sum(g.astype(F32) for g in got_keep), got_give]


def summed_in_pair(x):
    mine = x.astype(BF16)
    theirs = paired(mine, "z_hi", 1).astype(F32)
    half = x.shape[0] // 2
    return mine.astype(F32) + jnp.concatenate([theirs[half:], theirs[:half]], 0)


def two_blocks(give, keep, gains, weights):
    rows = give.shape[0]
    there = paired(jnp.concatenate([give, keep], 0), "z_hi", 1)
    give = jnp.concatenate([give, there[:rows]], 0)
    keep = jnp.concatenate([keep, there[rows:]], 0)
    column_keep, got_give = block(
        doubled(message(give, gains[0]), 3), lambda: doubled(message(keep, gains[0]), 3), *weights[0], False
    )
    keep = keep + summed_in_pair(halved(column_keep, 3, *got_give[1:]))
    give = give + summed_in_pair(halved(sum(g.astype(F32) for g in got_give), 3))
    column_give, got_keep = block(
        doubled(message(keep, gains[1]), 3), lambda: doubled(message(give, gains[1]), 3), *weights[1], True
    )
    give = give[:rows] + halved(halved(column_give, 3), 1)
    keep = keep[:rows] + halved(halved(sum(g.astype(F32) for g in got_keep), 3), 1)
    return give, keep


def stacked(gate, up, first):
    def kernel(first_ref, gate_ref, up_ref, out_ref, sems):
        copies = []
        place = 0
        for skip, size in ((0, MAIN), (MAIN, TAIL)):
            for ref in (gate_ref, up_ref):
                rows = pl.ds(pl.multiple_of(first_ref[0] + skip, 16), size)
                copies.append(
                    pltpu.make_async_copy(ref.at[rows], out_ref.at[pl.ds(place, size)], sems.at[len(copies)])
                )
                place += size
        for copy in copies:
            copy.start()
        for copy in copies:
            copy.wait()

    return pl.pallas_call(
        kernel,
        in_specs=[pl.BlockSpec(memory_space=pltpu.SMEM), IN_HBM, IN_HBM],
        out_specs=IN_VMEM,
        out_shape=jax.ShapeDtypeStruct((WIDE, gate.shape[1]), BF16),
        scratch_shapes=[pltpu.SemaphoreType.DMA((4,))],
        compiler_params=pltpu.CompilerParams(vmem_limit_bytes=VMEM_BYTES),
    )(
        first.astype(jnp.int32).reshape(1),
        *(pltpu.with_memory_space_constraint(w, pltpu.HBM) for w in (gate, up)),
    )


def per_device(
    tokens,
    gain_first,
    gate_first,
    up_first,
    down_first,
    gain_second,
    gate_second,
    up_second,
    down_second,
):
    core, z_lo = lax.axis_index("section"), lax.axis_index("z_lo")
    width = tokens.shape[1]
    rows = tokens.shape[0] // RING
    part = rows // 2

    gains = jnp.concatenate([gain_first[None], gain_second[None], jnp.zeros((6, width), F32)], 0)
    leaving = jnp.concatenate(
        [tokens.reshape(RING, rows, width), jnp.broadcast_to(gains[None], (RING, *gains.shape))], 1
    )
    came = jnp.concatenate(jnp.split(lax.all_to_all(leaving, "y", 0, 0, tiled=True), RING, 0), 2)[0]
    keep = lax.dynamic_slice_in_dim(came, z_lo * part, part, 0)
    give = lax.dynamic_slice_in_dim(came, (1 - z_lo) * part, part, 0)

    def whole(upper, down):
        return (
            lax.all_gather(upper, ("section", "y"), axis=0, tiled=True),
            lax.all_gather(down, ("y", "section"), axis=0, tiled=True),
        )

    first = core * UNITS
    lower_first = lax.dynamic_slice_in_dim(down_first, first, UNITS, 0)
    weights_first = whole(stacked(gate_first.T, up_first.T, first), lower_first)
    weights_second = whole(stacked(gate_second.T, up_second.T, jnp.zeros_like(first)), down_second)

    gains = came[rows : rows + 1], came[rows + 1 : rows + 2]
    give, keep = two_blocks(give, keep, gains, (weights_first, weights_second))

    whole_rows = jnp.where(z_lo == 0, jnp.concatenate([keep, give], 0), jnp.concatenate([give, keep], 0))
    back = jnp.stack(jnp.split(whole_rows, RING, 1), 0)
    return lax.all_to_all(back, "y", 0, 0, tiled=True).reshape(tokens.shape)


def solution(mesh):
    axes = ("section", "x", "z_hi", "y", "z_lo")
    split = Mesh(mesh.devices.reshape(2, RING, RING, RING, 2), axes)
    hid, mod = ("x", "z_hi"), ("y", "z_lo")
    both = ("section", *hid)
    return jax.shard_map(
        per_device,
        mesh=split,
        in_specs=(
            P(both, mod),
            P(mod),
            P(mod, hid),
            P(mod, hid),
            P(hid, mod),
            P(mod),
            P(mod, both),
            P(mod, both),
            P(both, mod),
        ),
        out_specs=P(both, mod),
        check_vma=False,
    )
```

```python
import jax
import jax.numpy as jnp
from jax import lax
from jax.experimental import pallas as pl
from jax.experimental.pallas import tpu as pltpu
from jax.sharding import Mesh
from jax.sharding import PartitionSpec as P

D = 5120
RING = 4
AHEAD = (2, 1, 3)
LANES = 128
epsilon = 1e-06
BF16 = jnp.bfloat16
F32 = jnp.float32

MAIN, TAIL = 384, 48
UNITS = MAIN + TAIL
WIDE = 2 * UNITS
WIDE_PAD = 896
ACT_PAD = 512
SQUARES = 2 * TAIL
PIECES = 3
VMEM_BYTES = 24 * 1024 * 1024


def shifted(x, axis, distance):
    size = lax.axis_size(axis)
    return lax.ppermute(x, axis, [(i, (i + distance) % size) for i in range(size)])


def after(xs, *others):
    anywhere = pl.BlockSpec(memory_space=pl.ANY)
    return pl.pallas_call(
        lambda *refs: None,
        out_shape=[jax.ShapeDtypeStruct(x.shape, x.dtype) for x in xs],
        in_specs=[anywhere] * (len(xs) + len(others)),
        out_specs=[anywhere] * len(xs),
        input_output_aliases={i: i for i in range(len(xs))},
    )(*xs, *others)


def from_behind(x, axis):
    got = {d: shifted(x, axis, d) for d in AHEAD}
    return [x, got[1], got[2], got[3]]


def to_owners(blocks, axis):
    return [blocks[0]] + [shifted(blocks[d], axis, -d) for d in AHEAD]


def paired(x, axis, flip):
    return lax.ppermute(x, axis, [(i, i ^ flip) for i in range(RING)])


def doubled(x, flip):
    return jnp.concatenate([x, paired(x, "z_hi", flip)], 0)


def halved(x, flip, *others):
    half = x.shape[0] // 2
    here = x[:half]
    if others:
        (here,) = after([here], *others)
    return here + paired(x[half:].astype(BF16), "z_hi", flip).astype(F32)


def three_pieces(x):
    high = lax.reduce_precision(x, 8, 7)
    middle = lax.reduce_precision(x - high, 8, 7)
    low = x - high - middle
    return [high.astype(BF16), middle.astype(BF16), low.astype(BF16)]


def message(v, gain):
    squares = jnp.sum(v * v, axis=1, keepdims=True)
    pieces = three_pieces(squares)
    blank = jnp.zeros((v.shape[0], LANES), BF16)
    return jnp.concatenate(
        [(v * gain).astype(BF16), blank[:, :SQUARES], *pieces, blank[:, : LANES - SQUARES - PIECES]], 1
    )


IN_VMEM = pl.BlockSpec(memory_space=pltpu.VMEM)
IN_HBM = pl.BlockSpec(memory_space=pltpu.HBM)


def fetched(w_ref, held, sems):
    pieces, size, _ = held.shape
    copies = [
        pltpu.make_async_copy(w_ref.at[pl.ds(i * size, size)], held.at[i], sems.at[i]) for i in range(pieces)
    ]
    for copy in copies:
        copy.start()

    def wait(i):
        copies[i].wait()
        return held[i]

    return wait


def partials(blocks, weights):
    rows, width = blocks[0].shape
    total_rows = RING * rows
    step = weights.shape[1]
    depth = RING * step
    pieces = 2 * RING

    def kernel(*refs):
        x_refs, (w_ref, out_ref, held, x_all, total, sems) = refs[:RING], refs[RING:]
        piece = fetched(w_ref, held, sems)
        for d in range(RING):
            x_all[d * rows : (d + 1) * rows, :] = x_refs[d][...]
        lane = lax.broadcasted_iota(jnp.int32, (total_rows, LANES), 1)
        head = WIDE_PAD - LANES
        for j in range(2):
            for y in range(RING):
                term = lax.dot_general(
                    x_all[:, y * step : (y + 1) * step],
                    piece(j * RING + y),
                    (((1,), (1,)), ((), ())),
                    preferred_element_type=F32,
                )
                total[:, :WIDE] = term if y == 0 else total[:, :WIDE] + term
            first = j * WIDE_PAD
            out_ref[:, first : first + head] = total[:, :head].astype(BF16)
            other = x_all[:, depth:].astype(F32) if j else jnp.zeros((total_rows, LANES), F32)
            out_ref[:, first + head : first + WIDE_PAD] = jnp.where(lane < SQUARES, total[:, head:], other).astype(BF16)

    return pl.pallas_call(
        kernel,
        in_specs=[IN_VMEM] * RING + [IN_HBM],
        out_specs=IN_VMEM,
        out_shape=jax.ShapeDtypeStruct((total_rows, 2 * WIDE_PAD), BF16),
        scratch_shapes=[
            pltpu.VMEM((pieces, WIDE, step), BF16),
            pltpu.VMEM((total_rows, width), BF16),
            pltpu.VMEM((total_rows, WIDE_PAD), F32),
            pltpu.SemaphoreType.DMA((pieces,)),
        ],
        compiler_params=pltpu.CompilerParams(vmem_limit_bytes=VMEM_BYTES),
        cost_estimate=pl.CostEstimate(
            flops=4 * total_rows * depth * WIDE, bytes_accessed=weights.size * 2, transcendentals=0
        ),
    )(*blocks, pltpu.with_memory_space_constraint(weights, pltpu.HBM))


def down_terms(act_ref, piece, out_refs):
    rows, width = out_refs[0].shape
    width //= RING
    for y in range(RING):
        w = piece(y)
        out = jnp.dot(act_ref[:, :UNITS], w[:UNITS], preferred_element_type=F32)
        out += jnp.dot(act_ref[:, ACT_PAD : ACT_PAD + UNITS], w[UNITS:], preferred_element_type=F32)
        for d in range(RING):
            out_refs[d][:, y * width : (y + 1) * width] = out[d * rows : (d + 1) * rows].astype(BF16)


def down_call(kernel, operands, lower, results, transcendentals):
    rows = operands[0].shape[0]
    width = lower.shape[1]
    shapes = results + [jax.ShapeDtypeStruct((rows // RING, RING * width), BF16)] * RING
    return pl.pallas_call(
        kernel,
        in_specs=[IN_VMEM] * len(operands) + [IN_HBM],
        out_specs=[IN_VMEM] * len(shapes),
        out_shape=shapes,
        scratch_shapes=[pltpu.VMEM((RING, 2 * UNITS, width), BF16), pltpu.SemaphoreType.DMA((RING,))],
        compiler_params=pltpu.CompilerParams(vmem_limit_bytes=VMEM_BYTES),
        cost_estimate=pl.CostEstimate(
            flops=2 * rows * lower.size, bytes_accessed=lower.size * 2, transcendentals=transcendentals
        ),
    )(*operands, pltpu.with_memory_space_constraint(lower, pltpu.HBM))


def activated_down(kept, got, lower):
    rows = kept.shape[0]

    def kernel(kept_ref, got_ref, w_ref, act_ref, *refs):
        out_refs, (held, sems) = refs[:RING], refs[RING:]
        piece = fetched(w_ref, held, sems)

        def both(first, columns):
            part = pl.ds(first, columns)
            return kept_ref[:, part].astype(F32) + got_ref[:, part].astype(F32)

        head = WIDE_PAD - LANES
        last = both(WIDE_PAD + head, LANES)
        lane = lax.broadcasted_iota(jnp.int32, last.shape, 1)
        carried = (lane >= SQUARES) & (lane < SQUARES + PIECES)
        squares = jnp.sum(jnp.where(carried, last, 0.0), axis=1, keepdims=True)
        scale = lax.rsqrt(squares / D + epsilon)

        def unit(gate, up):
            gate = gate * scale
            return gate / (1.0 + jnp.exp(-gate)) * (up * scale)

        for j in range(2):
            first, place = j * WIDE_PAD, j * ACT_PAD
            act_ref[:, place : place + MAIN] = unit(both(first, MAIN), both(first + MAIN, MAIN)).astype(BF16)
            tile = last if j else both(head, LANES)
            tails = unit(tile, pltpu.roll(tile, LANES - TAIL, 1))
            act_ref[:, place + MAIN : place + ACT_PAD] = jnp.where(lane < TAIL, tails, 0.0).astype(BF16)
        down_terms(act_ref, piece, out_refs)

    act, *out = down_call(
        kernel, [kept, got], lower, [jax.ShapeDtypeStruct((rows, 2 * ACT_PAD), BF16)], rows * WIDE
    )
    return act, out


def down_product(act, lower):
    def kernel(act_ref, w_ref, *refs):
        out_refs, (held, sems) = refs[:RING], refs[RING:]
        down_terms(act_ref, fetched(w_ref, held, sems), out_refs)

    return list(down_call(kernel, [act], lower, [], 0))


def block(column_give, keep, weights, lower, last):
    wide_give = from_behind(column_give, "x")
    given = partials(wide_give, weights)
    (column_keep,) = after([keep()], *([given] if last else wide_give[1:]))
    wide_keep = from_behind(column_keep, "x")
    got = shifted(given, "z_lo", 1)
    kept = partials(wide_keep, weights)
    if not last:
        (lower,) = after([pltpu.with_memory_space_constraint(lower, pltpu.HBM)], kept[:16, :LANES])
    act_keep, out_keep = activated_down(kept, got, lower)
    act_give = shifted(act_keep, "z_lo", 1)
    got_keep = to_owners(out_keep, "x")
    out_give = down_product(act_give, lower)
    (got_keep[2],) = after([got_keep[2]], out_give[0])
    got_give = to_owners(out_give, "x")
    return [sum(g.astype(F32) for g in got_keep), got_give]


def two_blocks(give, keep, gains, weights):
    column_keep, got_give = block(
        doubled(doubled(message(give, gains[0]), 1), 3),
        lambda: doubled(doubled(message(keep, gains[0]), 1), 3),
        *weights[0],
        False,
    )
    keep = keep + halved(halved(column_keep, 3, *got_give[1:]), 1)
    rest = halved(sum(g.astype(F32) for g in got_give), 3)
    two = doubled(message(keep, gains[1]), 1)
    column = doubled(two, 3)
    give = give + halved(rest, 1)
    column_give, got_keep = block(
        column, lambda: doubled(doubled(message(give, gains[1]), 1), 3), *weights[1], True
    )
    give = give + halved(halved(column_give, 3), 1)
    keep = keep + halved(halved(sum(g.astype(F32) for g in got_keep), 3), 1)
    return give, keep


def stacked(gate, up, first):
    def kernel(first_ref, gate_ref, up_ref, out_ref, sems):
        copies = []
        place = 0
        for skip, size in ((0, MAIN), (MAIN, TAIL)):
            for ref in (gate_ref, up_ref):
                rows = pl.ds(pl.multiple_of(first_ref[0] + skip, 16), size)
                copies.append(
                    pltpu.make_async_copy(ref.at[rows], out_ref.at[pl.ds(place, size)], sems.at[len(copies)])
                )
                place += size
        for copy in copies:
            copy.start()
        for copy in copies:
            copy.wait()

    return pl.pallas_call(
        kernel,
        in_specs=[pl.BlockSpec(memory_space=pltpu.SMEM), IN_HBM, IN_HBM],
        out_specs=IN_VMEM,
        out_shape=jax.ShapeDtypeStruct((WIDE, gate.shape[1]), BF16),
        scratch_shapes=[pltpu.SemaphoreType.DMA((4,))],
        compiler_params=pltpu.CompilerParams(vmem_limit_bytes=VMEM_BYTES),
    )(
        first.astype(jnp.int32).reshape(1),
        *(pltpu.with_memory_space_constraint(w, pltpu.HBM) for w in (gate, up)),
    )


def per_device(
    tokens,
    gain_first,
    gate_first,
    up_first,
    down_first,
    gain_second,
    gate_second,
    up_second,
    down_second,
):
    core, z_lo = lax.axis_index("section"), lax.axis_index("z_lo")
    width = tokens.shape[1]
    rows = tokens.shape[0] // RING
    part = rows // 2

    gains = jnp.concatenate([gain_first[None], gain_second[None], jnp.zeros((6, width), F32)], 0)
    leaving = jnp.concatenate(
        [tokens.reshape(RING, rows, width), jnp.broadcast_to(gains[None], (RING, *gains.shape))], 1
    )
    came = jnp.concatenate(jnp.split(lax.all_to_all(leaving, "y", 0, 0, tiled=True), RING, 0), 2)[0]
    keep = lax.dynamic_slice_in_dim(came, z_lo * part, part, 0)
    give = lax.dynamic_slice_in_dim(came, (1 - z_lo) * part, part, 0)

    def whole(upper, down):
        return (
            lax.all_gather(upper, ("section", "y"), axis=0, tiled=True),
            lax.all_gather(down, ("y", "section"), axis=0, tiled=True),
        )

    first = core * UNITS
    lower_first = lax.dynamic_slice_in_dim(down_first, first, UNITS, 0)
    weights_first = whole(stacked(gate_first.T, up_first.T, first), lower_first)
    weights_second = whole(stacked(gate_second.T, up_second.T, jnp.zeros_like(first)), down_second)

    gains = came[rows : rows + 1], came[rows + 1 : rows + 2]
    give, keep = two_blocks(give, keep, gains, (weights_first, weights_second))

    whole_rows = jnp.where(z_lo == 0, jnp.concatenate([keep, give], 0), jnp.concatenate([give, keep], 0))
    back = jnp.stack(jnp.split(whole_rows, RING, 1), 0)
    return lax.all_to_all(back, "y", 0, 0, tiled=True).reshape(tokens.shape)


def solution(mesh):
    axes = ("section", "x", "z_hi", "y", "z_lo")
    split = Mesh(mesh.devices.reshape(2, RING, RING, RING, 2), axes)
    hid, mod = ("x", "z_hi"), ("y", "z_lo")
    both = ("section", *hid)
    return jax.shard_map(
        per_device,
        mesh=split,
        in_specs=(
            P(both, mod),
            P(mod),
            P(mod, hid),
            P(mod, hid),
            P(hid, mod),
            P(mod),
            P(mod, both),
            P(mod, both),
            P(both, mod),
        ),
        out_specs=P(both, mod),
        check_vma=False,
    )
```
